32 devices in a mesh: dp: 4 (over y, core), mp: 8 (over z, x).
Axes of the slice: x: 2, y: 2, z: 4, core: 2. Of those that a mesh axis runs over, the one named last changes fastest.
Arguments:
- activations: bfloat16 [1024, 8192], P('dp', 'mp'), may hold values from -40 to 40
- out_grads: bfloat16 [1024, 8192], P('dp', 'mp'), may hold values from -40 to 40
- basis_in: bfloat16 [8192, 8192], P(None, 'mp'), may hold values from -1 to 1
- basis_out: bfloat16 [8192, 8192], P(None, 'mp'), may hold values from -1 to 1
- grad_eigen: bfloat16 [8192, 8192], P('mp', 'dp'), may hold values from -8 to 8
Outputs:
- precond: bfloat16 [8192, 8192], P(('mp', 'dp'))
The draws below stay inside these ranges and needn't reach their ends.
All inputs are finite; a program needn't handle non-finite values.
Results may differ from the reference program's by a relative error of at most 0.015.
Values may be sent and summed in bfloat16 or wider, within the bound.
A program may use at most 128 MiB of HBM per device.

```python
import jax
import jax.numpy as jnp
from jax import lax

D = 8192
TOK_DEV = 256
TOKENS = 1024
N_DP = 4


def basis_draw(key, salt_value):
    key_basis = jax.random.fold_in(key, salt_value)
    values = jnp.clip(jax.random.normal(key_basis, (D, D), jnp.float32), -4.0, 4.0) * D ** (-0.5)
    return values.astype(jnp.bfloat16)


def drawn_rows(key, salt_basis, salt_own, coef_scale, rising):
    basis_full = basis_draw(key, salt_basis).astype(jnp.float32)
    key_own = jax.random.fold_in(key, salt_own)
    key_blocks = jax.random.fold_in(key_own, 3)
    key_values = jax.random.fold_in(key_own, 7)
    key_rows = jax.random.fold_in(key_own, 13)
    token_block = jax.random.randint(key_blocks, (TOKENS, 1), 0, 16)
    column_block = (jnp.arange(D) // (D // 16)).reshape(1, D)
    jitter = jnp.clip(jax.random.normal(key_values, (TOKENS, D), jnp.float32), -4.0, 4.0)
    inside = (column_block == token_block).astype(jnp.float32)
    row_scale = 2.0 ** (jax.random.uniform(key_rows, (TOKENS, 1), jnp.float32) - 0.5)
    if rising:
        position = jnp.arange(TOKENS, dtype=jnp.float32).reshape(TOKENS, 1) / TOKENS
        row_scale = row_scale * 3.0 ** position
    coefficients = jitter * inside * coef_scale * row_scale
    aligned = jnp.dot(coefficients, basis_full.T, precision=lax.Precision.HIGHEST)
    return jnp.clip(aligned, -40.0, 40.0).astype(jnp.bfloat16)


def draw_basis_in(key, part):
    return basis_draw(key, 101)


def draw_basis_out(key, part):
    return basis_draw(key, 202)


def draw_activations(key, part):
    return drawn_rows(key, 101, 303, 2.0, True)


def draw_out_grads(key, part):
    return drawn_rows(key, 202, 404, 3.0, False)


def steps_of(own_key, shape, shards, low, top_value):
    factor_of = 1.0
    for axis_at, parts in shards:
        steps = jax.random.uniform(jax.random.fold_in(jax.random.fold_in(own_key, 6), axis_at), (parts,), jnp.float32, low / len(shards), top_value / len(shards))
        factor_of = factor_of * jnp.repeat(jnp.exp(steps), shape[axis_at] // parts).reshape((-1,) + (1,) * (len(shape) - 1 - axis_at))
    return factor_of


def noise(rng, extent, deviation, limit, split=(), kind=jnp.bfloat16):
    values = deviation * jax.random.normal(rng, extent, jnp.float32)
    if split:
        values = values * steps_of(rng, extent, split, -0.22, 0.18)
    return jnp.clip(values, -limit, limit).astype(kind)


def setup_inputs(seed: int = 0) -> dict:
    seeds = jax.random.split(jax.random.key(seed), 6)
    activations = draw_activations(jax.random.fold_in(seeds[5], 71), 0)
    out_grads = draw_out_grads(jax.random.fold_in(seeds[5], 71), 0)
    basis_in = draw_basis_in(jax.random.fold_in(seeds[5], 71), 0)
    basis_out = draw_basis_out(jax.random.fold_in(seeds[5], 71), 0)
    grad_eigen = noise(seeds[4], (D, D), 2.0, 8.0, ((0, 8), (1, 4)))
    return dict(activations=activations, out_grads=out_grads, basis_in=basis_in, basis_out=basis_out, grad_eigen=grad_eigen)


damping = 0.1


def reference(activations, out_grads, basis_in, basis_out, grad_eigen):
    proj_in = jnp.dot(activations, basis_in, preferred_element_type=jnp.float32)
    squares_in = (proj_in * proj_in).astype(jnp.bfloat16)
    proj_out = jnp.dot(out_grads, basis_out, preferred_element_type=jnp.float32)
    squares_out = (proj_out * proj_out).astype(jnp.bfloat16)
    groups_in = squares_in.reshape(N_DP, TOK_DEV, D)
    groups_out = squares_out.reshape(N_DP, TOK_DEV, D)

    def accumulate(summed, operands):
        left_rows, right_rows = operands
        partial_value = lax.dot_general(left_rows, right_rows, (((0,), (0,)), ((), ())), preferred_element_type=jnp.float32)
        partial_value = lax.optimization_barrier(partial_value.astype(jnp.bfloat16)).astype(jnp.float32)
        return summed + partial_value, None

    summed, unused = lax.scan(accumulate, jnp.zeros((D, D), jnp.float32), (groups_in, groups_out))
    scaling = summed / (TOK_DEV * N_DP)
    return (grad_eigen.astype(jnp.float32) / (scaling + damping)).astype(jnp.bfloat16)
```

```python
import functools

import jax
import jax.numpy as jnp
from jax import lax
from jax.experimental import pallas as pl
from jax.experimental.pallas import tpu as pltpu
from jax.sharding import PartitionSpec as P

damping = 0.1
MESH = pl.DeviceIdType.MESH
OUT, IN, SQ = 0, 1, 2
UP, DOWN = 0, 1


def projector(basis, piece):
    return jnp.dot(piece, basis, preferred_element_type=jnp.float32)


def general(activations, out_grads, basis_in, basis_out, grad_eigen):
    tok_rows = activations.shape[0]
    groups = lax.axis_size("dp")
    proj_in = projector(basis_in, lax.all_gather(activations, "mp", axis=1, tiled=True))
    proj_out = projector(basis_out, lax.all_gather(out_grads, "mp", axis=1, tiled=True))
    squares_in = (proj_in * proj_in).astype(jnp.bfloat16)
    squares_out = (proj_out * proj_out).astype(jnp.bfloat16)
    partial_sums = lax.dot_general(
        squares_in,
        lax.all_gather(squares_out, "mp", axis=1, tiled=True),
        (((0,), (0,)), ((), ())),
        preferred_element_type=jnp.float32,
    )
    summed = lax.psum_scatter(
        partial_sums.astype(jnp.bfloat16), "dp", scatter_dimension=1, tiled=True
    ).astype(jnp.float32)
    scaling = summed / (tok_rows * groups)
    block_result = (grad_eigen.astype(jnp.float32) / (scaling + damping)).astype(jnp.bfloat16)
    return lax.all_to_all(block_result, "dp", split_axis=0, concat_axis=1, tiled=True)


def kernel(
    act, og, basis_in, basis_out, grad, out,
    held, squares, sq_in, sq_in_send, grads, basis, acc,
    load_sem, zsend, zrecv, xsend, xrecv, ysend, yrecv, csend, crecv, ysend2, gsend, grecv, isend, irecv,
):
    tok, feat = act.shape
    n_mp, n_dp = held.shape[1], squares.shape[0]
    n_z = n_mp // 2
    rows = out.shape[0]
    width = grad.shape[1]
    d, m = lax.axis_index("dp"), lax.axis_index("mp")
    y, c = d // 2, d % 2
    z, x = m // 2, m % 2
    y_peer, c_peer, x_peer = (1 - y) * 2 + c, y * 2 + 1 - c, z * 2 + 1 - x
    others = [(d + i) % n_dp for i in range(1, n_dp)]

    def slot_of(step, way, other_x=False):
        at = z - step if way == UP else z + step
        return at * 2 + ((1 - x) if other_x else x)

    def there(step, way):
        return z >= step if way == UP else z + step < n_z

    def ways(step):
        return (UP,) if step == 0 else (UP, DOWN)

    def buffer(a, slot, owner=None):
        if a == SQ:
            return squares.at[d if owner is None else owner, slot]
        return held.at[a, slot]

    def copy(ref, send, recv, target):
        return pltpu.make_async_remote_copy(
            src_ref=ref, dst_ref=ref, send_sem=send, recv_sem=recv,
            device_id=target, device_id_type=MESH,
        )

    def z_copy(a, step, way, slot):
        target = m + 2 if way == UP else m - 2
        return copy(buffer(a, slot), zsend.at[a, step, way], zrecv.at[a, step, way], {"mp": target})

    def x_copy(a, step, way, slot):
        return copy(buffer(a, slot), xsend.at[a, step, way], xrecv.at[a, step, way], {"mp": x_peer})

    def y_copy(step, way, other_x, owner):
        ref = buffer(SQ, slot_of(step, way, other_x), owner)
        return copy(ref, ysend.at[step, way, other_x], yrecv.at[step, way, other_x], {"dp": y_peer})

    def c_copy(step, way, other_x, far, owner):
        ref = buffer(SQ, slot_of(step, way, other_x), owner)
        return copy(ref, csend.at[step, way, other_x, far], crecv.at[step, way, other_x, far], {"dp": c_peer})

    def can_pass(step, way):
        return (z < n_z - 1) if way == UP else (z > 0)

    def send_z(a, step, way):
        @pl.when(can_pass(step, way))
        def _():
            z_copy(a, step, way, slot_of(step, way)).start()

    def spread(step, way, other_x):
        y_copy(step, way, other_x, d).start()
        c_copy(step, way, other_x, 0, d).start()

    def first(a):
        send_z(a, 0, UP)
        send_z(a, 0, DOWN)
        x_copy(a, 0, UP, m).start()
        if a == SQ:
            spread(0, UP, 0)

    def pass_on(a, step):
        for way in ways(step):
            @pl.when(there(step, way))
            def _():
                z_copy(a, step - 1, way, slot_of(step, way)).wait_recv()
                if step < n_z - 1:
                    send_z(a, step, way)
                x_copy(a, step, way, slot_of(step, way)).start()
                if a == SQ:
                    spread(step, way, 0)

    def from_x(a, step):
        for way in ways(step):
            @pl.when(there(step, way))
            def _():
                x_copy(a, step, way, slot_of(step, way, True)).wait_recv()
                if a == SQ:
                    spread(step, way, 1)

    def from_y(step):
        for way in ways(step):
            @pl.when(there(step, way))
            def _():
                for other_x in (0, 1):
                    y_copy(step, way, other_x, y_peer).wait_recv()
                    c_copy(step, way, other_x, 1, y_peer).start()

    def load_basis(source):
        return [
            pltpu.make_async_copy(source.at[pl.ds(i * feat, feat), :], basis.at[i], load_sem.at[i])
            for i in range(n_mp)
        ]

    def multiply(a, near):
        tile = 256

        def one(i, carry):
            far = jnp.abs(i // 2 - z)
            wanted = far <= 1 if near else far > 1

            @pl.when(wanted)
            def _():
                @pl.loop(0, acc.shape[1] // tile)
                def _(j):
                    cols = pl.ds(pl.multiple_of(j * tile, tile), tile)
                    acc[:, cols] += jnp.dot(
                        held[a, i], basis[i, :, cols], preferred_element_type=jnp.float32
                    )
            return carry

        lax.fori_loop(0, n_mp, one, 0)

    own_out = pltpu.make_async_copy(og, held.at[OUT, m], load_sem.at[n_mp])
    own_in = pltpu.make_async_copy(act, held.at[IN, m], load_sem.at[n_mp + 1])
    own_grad = pltpu.make_async_copy(
        grad.at[pl.ds(pl.multiple_of(d * rows, rows), rows), :], grads.at[d], load_sem.at[n_mp + 2]
    )
    own_out.start()
    own_in.start()
    own_grad.start()
    for one in load_basis(basis_out):
        one.start()

    barrier = pltpu.get_barrier_semaphore()
    peers = [{"mp": x_peer}] + [{"dp": other} for other in others]
    for peer in peers:
        pl.semaphore_signal(barrier, inc=1, device_id=peer, device_id_type=MESH)

    @pl.when(z > 0)
    def _():
        pl.semaphore_signal(barrier, inc=1, device_id={"mp": m - 2}, device_id_type=MESH)

    @pl.when(z < n_z - 1)
    def _():
        pl.semaphore_signal(barrier, inc=1, device_id={"mp": m + 2}, device_id_type=MESH)

    inner = (z > 0).astype(jnp.int32) + (z < n_z - 1).astype(jnp.int32)
    pl.semaphore_wait(barrier, len(peers) + inner)

    def grad_copy(k, other):
        return pltpu.make_async_remote_copy(
            src_ref=grad.at[pl.ds(pl.multiple_of(other * rows, rows), rows), :], dst_ref=grads.at[d],
            send_sem=gsend.at[k], recv_sem=grecv.at[k],
            device_id={"dp": other}, device_id_type=MESH,
        )

    def in_copy(k, other):
        return pltpu.make_async_remote_copy(
            src_ref=sq_in_send.at[other], dst_ref=sq_in.at[d],
            send_sem=isend.at[k], recv_sem=irecv.at[k],
            device_id={"dp": other}, device_id_type=MESH,
        )

    own_out.wait()
    first(OUT)
    for k, other in enumerate(others):
        grad_copy(k, other).start()
    own_in.wait()
    for step in range(1, n_z):
        pass_on(OUT, step)
    first(IN)

    acc[...] = jnp.zeros_like(acc)
    for one in load_basis(basis_out):
        one.wait()
    for step in (0, 1):
        from_x(OUT, step)
    multiply(OUT, True)
    for step in range(2, n_z):
        from_x(OUT, step)
    multiply(OUT, False)
    squares[d, m] = (acc[...] * acc[...]).astype(jnp.bfloat16)
    first(SQ)
    for one in load_basis(basis_in):
        one.start()
    acc[...] = jnp.zeros_like(acc)

    for step in range(1, n_z):
        from_x(SQ, step - 1)
        pass_on(SQ, step)
        pass_on(IN, step)
        if step > 1:
            from_y(step - 2)
    from_x(SQ, n_z - 1)

    for one in load_basis(basis_in):
        one.wait()
    for step in (0, 1):
        from_x(IN, step)
    multiply(IN, True)
    for step in range(2, n_z):
        from_x(IN, step)
    multiply(IN, False)
    for k in range(n_dp):
        part = acc[:, k * rows:(k + 1) * rows]
        sq_in_send[k] = (part * part).T.astype(jnp.bfloat16)
    for k, other in enumerate(others):
        in_copy(k, other).start()
    sq_in[d] = sq_in_send[d]

    for step in range(n_z - 2, n_z):
        from_y(step)

    own_grad.wait()
    for k, other in enumerate(others):
        back = (d + n_dp - k - 1) % n_dp
        pltpu.make_async_remote_copy(
            src_ref=grads.at[back], dst_ref=grads.at[back], send_sem=gsend.at[k], recv_sem=grecv.at[k],
            device_id={"dp": other}, device_id_type=MESH,
        ).wait_recv()
        pltpu.make_async_remote_copy(
            src_ref=sq_in.at[back], dst_ref=sq_in.at[back], send_sem=isend.at[k], recv_sem=irecv.at[k],
            device_id={"dp": other}, device_id_type=MESH,
        ).wait_recv()
    for step in range(n_z):
        for way in ways(step):
            @pl.when(there(step, way))
            def _():
                for other_x in (0, 1):
                    c_copy(step, way, other_x, 0, c_peer).wait_recv()
                    c_copy(step, way, other_x, 1, (1 - y) * 2 + 1 - c).wait_recv()

    tile = 256
    per_block, per_grad = feat // tile, width // tile

    @pl.loop(0, out.shape[1] // tile)
    def _(t):
        block, cols = t // per_block, pl.ds(pl.multiple_of((t % per_block) * tile, tile), tile)
        total = jnp.zeros((rows, tile), jnp.float32)
        for k in range(n_dp):
            total += jnp.dot(sq_in[k], squares[k, block, :, cols], preferred_element_type=jnp.float32)
        scaling = total / (tok * n_dp)
        cols_g = pl.ds(pl.multiple_of((t % per_grad) * tile, tile), tile)
        top = grads[t // per_grad, :, cols_g].astype(jnp.float32)
        out[:, pl.ds(pl.multiple_of(t * tile, tile), tile)] = (top / (scaling + damping)).astype(out.dtype)

    for k, other in enumerate(others):
        grad_copy(k, other).wait_send()
        in_copy(k, other).wait_send()
    for step in range(n_z):
        for way in ways(step):
            @pl.when(there(step, way))
            def _():
                for a in (OUT, IN, SQ):
                    x_copy(a, step, way, slot_of(step, way)).wait_send()
                for other_x in (0, 1):
                    y_copy(step, way, other_x, d).wait_send()
                    c_copy(step, way, other_x, 0, d).wait_send()
                    c_copy(step, way, other_x, 1, y_peer).wait_send()
        if step < n_z - 1:
            for way in (UP, DOWN):
                @pl.when(there(step, way) & can_pass(step, way))
                def _():
                    for a in (OUT, IN, SQ):
                        z_copy(a, step, way, slot_of(step, way)).wait_send()


def per_device(activations, out_grads, basis_in, basis_out, grad_eigen):
    tok, feat = activations.shape
    n_dp, n_mp = lax.axis_size("dp"), lax.axis_size("mp")
    depth, cols = basis_in.shape
    height, width = grad_eigen.shape
    rows = height // n_dp
    n_z = n_mp // 2
    dma = pltpu.SemaphoreType.DMA
    spec = pl.BlockSpec(memory_space=pl.ANY)
    return pl.pallas_call(
        kernel,
        out_shape=jax.ShapeDtypeStruct((rows, depth), jnp.bfloat16),
        in_specs=[spec] * 5,
        out_specs=pl.BlockSpec(memory_space=pltpu.VMEM),
        scratch_shapes=[
            pltpu.VMEM((2, n_mp, tok, feat), jnp.bfloat16),
            pltpu.VMEM((n_dp, n_mp, tok, cols), jnp.bfloat16),
            pltpu.VMEM((n_dp, rows, tok), jnp.bfloat16),
            pltpu.VMEM((n_dp, rows, tok), jnp.bfloat16),
            pltpu.VMEM((n_dp, rows, width), jnp.bfloat16),
            pltpu.VMEM((n_mp, feat, cols), jnp.bfloat16),
            pltpu.VMEM((tok, cols), jnp.float32),
            dma((n_mp + 3,)),
            dma((3, n_z, 2)), dma((3, n_z, 2)),
            dma((3, n_z, 2)), dma((3, n_z, 2)),
            dma((n_z, 2, 2)), dma((n_z, 2, 2)),
            dma((n_z, 2, 2, 2)), dma((n_z, 2, 2, 2)),
            dma((n_dp,)),
            dma((n_dp,)), dma((n_dp,)),
            dma((n_dp,)), dma((n_dp,)),
        ],
        compiler_params=pltpu.CompilerParams(
            collective_id=0, has_side_effects=True, vmem_limit_bytes=60 * 1024 * 1024
        ),
        cost_estimate=pl.CostEstimate(
            flops=4 * tok * depth * cols + 2 * rows * tok * n_dp * depth,
            bytes_accessed=4 * depth * cols + 4 * height * width,
            transcendentals=0,
        ),
    )(activations, out_grads, basis_in, basis_out, grad_eigen)


def solution(mesh):
    placed = (P("dp", "mp"), P("dp", "mp"), P(None, "mp"), P(None, "mp"), P("mp", "dp"))
    routed = (mesh.shape["dp"], mesh.shape["mp"]) == (4, 8)
    return jax.shard_map(
        per_device if routed else general,
        mesh=mesh, in_specs=placed, out_specs=P(("mp", "dp"), None), check_vma=False,
    )
```

```python
import jax
import jax.numpy as jnp
from jax import lax
from jax.experimental import pallas as pl
from jax.experimental.pallas import tpu as pltpu
from jax.sharding import PartitionSpec as P

damping = 0.1
MESH = pl.DeviceIdType.MESH
OUT, IN, SQ = 0, 1, 2
UP, DOWN = 0, 1


def projector(basis, piece):
    return jnp.dot(piece, basis, preferred_element_type=jnp.float32)


def general(activations, out_grads, basis_in, basis_out, grad_eigen):
    tok_rows = activations.shape[0]
    groups = lax.axis_size("dp")
    proj_in = projector(basis_in, lax.all_gather(activations, "mp", axis=1, tiled=True))
    proj_out = projector(basis_out, lax.all_gather(out_grads, "mp", axis=1, tiled=True))
    squares_in = (proj_in * proj_in).astype(jnp.bfloat16)
    squares_out = (proj_out * proj_out).astype(jnp.bfloat16)
    partial_sums = lax.dot_general(
        squares_in,
        lax.all_gather(squares_out, "mp", axis=1, tiled=True),
        (((0,), (0,)), ((), ())),
        preferred_element_type=jnp.float32,
    )
    summed = lax.psum_scatter(
        partial_sums.astype(jnp.bfloat16), "dp", scatter_dimension=1, tiled=True
    ).astype(jnp.float32)
    scaling = summed / (tok_rows * groups)
    block_result = (grad_eigen.astype(jnp.float32) / (scaling + damping)).astype(jnp.bfloat16)
    return lax.all_to_all(block_result, "dp", split_axis=0, concat_axis=1, tiled=True)


def kernel(
    act, og, basis_in, basis_out, grad, out,
    held, squares, sq_in, sq_in_send, grads, basis, acc, result,
    load_sem, store_sem, zsend, zrecv, xsend, xrecv, dsend, drecv, ysend, yrecv, csend, crecv,
    gsend, grecv, isend, irecv,
):
    tok, feat = act.shape
    n_mp, n_dp = held.shape[1], squares.shape[0]
    n_z = n_mp // 2
    rows = out.shape[0]
    width = grad.shape[1]
    half = tok // 2
    d, m = lax.axis_index("dp"), lax.axis_index("mp")
    y, c = d // 2, d % 2
    z, x = m // 2, m % 2
    y_peer, c_peer, x_peer = (1 - y) * 2 + c, y * 2 + 1 - c, z * 2 + 1 - x
    diagonal = (1 - y) * 2 + 1 - c
    others = [(d + i) % n_dp for i in range(1, n_dp)]
    started = []

    def do(wanted, action):
        if wanted is True:
            action()
        else:
            pl.when(wanted)(action)

    def start(wanted, copy):
        started.append((wanted, copy))
        do(wanted, lambda: copy().start())

    def arrived(wanted, copy):
        do(wanted, lambda: copy().wait_recv())

    def both(one, other):
        if one is True:
            return other
        return one if other is True else one & other

    def slot_of(step, way, other_x):
        at = z - step if way == UP else z + step
        return at * 2 + ((1 - x) if other_x else x)

    def there(step, way):
        if step == 0:
            return True
        return z >= step if way == UP else z + step < n_z

    def ways(step):
        return (UP,) if step == 0 else (UP, DOWN)

    def can_pass(way):
        return z < n_z - 1 if way == UP else z > 0

    def paired(step, way, h):
        if h == 0 or step == 0:
            return False
        return z == step if way == UP else z + step == n_z - 1

    def alone(step, way, h):
        if h == 0 or step == 0:
            return there(step, way)
        return z > step if way == UP else z + step < n_z - 1

    def part(a, step, way, other_x, h, owner=None):
        slot = slot_of(step, way, other_x)
        lines = pl.ds(h * half, half)
        if a == SQ:
            return squares.at[d if owner is None else owner, slot, lines]
        return held.at[a, slot, lines]

    def remote(ref, send, recv, target):
        return pltpu.make_async_remote_copy(
            src_ref=ref, dst_ref=ref, send_sem=send, recv_sem=recv,
            device_id=target, device_id_type=MESH,
        )

    def z_copy(a, step, way, other_x, h):
        at = (a, step, way, other_x, h)
        target = m + 2 if way == UP else m - 2
        return remote(part(*at), zsend.at[at], zrecv.at[at], {"mp": target})

    def x_copy(a, step, way, h, other_x=0):
        at = (a, step, way, h)
        return remote(part(a, step, way, other_x, h), xsend.at[at], xrecv.at[at], {"mp": x_peer})

    def d_copy(h, other_x=0):
        return remote(part(SQ, 0, UP, other_x, h, y_peer), dsend.at[h], drecv.at[h], {"mp": x_peer})

    def y_copy(step, way, other_x, h, owner):
        at = (step, way, other_x, h)
        return remote(part(SQ, *at, owner), ysend.at[at], yrecv.at[at], {"dp": y_peer})

    def c_copy(step, way, other_x, h, far, owner):
        at = (step, way, other_x, h)
        return remote(part(SQ, *at, owner), csend.at[(far,) + at], crecv.at[(far,) + at], {"dp": c_peer})

    def send_z(a, step, way, other_x, h, wanted):
        if step < n_z - 1:
            start(both(wanted, can_pass(way)), lambda: z_copy(a, step, way, other_x, h))

    def send_x(a, step):
        for h in (0, 1):
            for way in ways(step):
                start(alone(step, way, h), lambda way=way, h=h: x_copy(a, step, way, h))

    def spread(step, way, other_x, h, wanted):
        if step > 0 or not other_x:
            start(wanted, lambda: y_copy(step, way, other_x, h, d))
        start(wanted, lambda: c_copy(step, way, other_x, h, 0, d))

    def first_z(a):
        for h in (0, 1):
            for way in (UP, DOWN):
                send_z(a, 0, way, 0, h, True)

    def along_z(a, step):
        for h in (0, 1):
            for way in (UP, DOWN):
                wanted = there(step, way)
                arrived(wanted, lambda: z_copy_in(a, step, way, 0, h))
                send_z(a, step, way, 0, h, wanted)
                if a == SQ:
                    spread(step, way, 0, h, wanted)

    def z_copy_in(a, step, way, other_x, h):
        ref = part(a, step, way, other_x, h)
        at = (a, step - 1, way, other_x, h)
        return remote(ref, zsend.at[at], zrecv.at[at], {"mp": x_peer})

    def pairs(a, step):
        for way in (UP, DOWN):
            wanted = paired(step, way, 1)
            arrived(wanted, lambda: z_copy_in(a, step, way, 1, 1))
            send_z(a, step, way, 1, 1, wanted)
            if a == SQ:
                spread(step, way, 1, 1, wanted)

    def from_x(a, step):
        for h in (0, 1):
            for way in ways(step):
                wanted = alone(step, way, h)
                arrived(wanted, lambda: x_copy(a, step, way, h, 1))
                if step == 0 and h == 1:
                    send_z(a, 0, UP, 1, h, z == 0)
                    send_z(a, 0, DOWN, 1, h, z == n_z - 1)
                if a == SQ:
                    spread(step, way, 1, h, wanted)

    def from_y(step):
        for other_x in (0, 1) if step > 0 else (0,):
            for h in (0, 1):
                for way in ways(step):
                    wanted = there(step, way)
                    arrived(wanted, lambda: y_copy(step, way, other_x, h, y_peer))
                    start(wanted, lambda way=way, other_x=other_x, h=h: c_copy(step, way, other_x, h, 1, y_peer))

    def from_core(step):
        for other_x in (0, 1):
            for h in (0, 1):
                for way in ways(step):
                    wanted = there(step, way)
                    arrived(wanted, lambda: c_copy(step, way, other_x, h, 0, c_peer))
                    arrived(wanted, lambda: c_copy(step, way, other_x, h, 1, diagonal))

    def load_basis(source):
        return [
            pltpu.make_async_copy(source.at[pl.ds(i * feat, feat), :], basis.at[i], load_sem.at[i])
            for i in range(n_mp)
        ]

    tile = 256

    def blocks_within(low, high, action):
        def one(i, carry):
            away = jnp.abs(i // 2 - z)
            pl.when((away >= low) & (away <= high))(lambda: action(i))
            return carry

        lax.fori_loop(0, n_mp, one, 0)

    def multiply(a, low, high):
        def block(i):
            @pl.loop(0, acc.shape[1] // tile)
            def _(j):
                cols = pl.ds(pl.multiple_of(j * tile, tile), tile)
                acc[:, cols] += jnp.dot(held[a, i], basis[i, :, cols], preferred_element_type=jnp.float32)

        blocks_within(low, high, block)

    def store(i):
        cols = pl.ds(pl.multiple_of(i * feat, feat), feat)
        return pltpu.make_async_copy(result.at[:, cols], out.at[:, cols], store_sem.at[i])

    def finish(low, high):
        per_grad = width // feat

        def block(i):
            @pl.loop(0, feat // tile)
            def _(j):
                cols = pl.ds(pl.multiple_of(j * tile, tile), tile)
                total = jnp.zeros((rows, tile), jnp.float32)
                for k in range(n_dp):
                    total += jnp.dot(sq_in[k], squares[k, i, :, cols], preferred_element_type=jnp.float32)
                scaling = total / (tok * n_dp)
                at_grad = pl.ds(pl.multiple_of((i % per_grad) * feat + j * tile, tile), tile)
                top = grads[i // per_grad, :, at_grad].astype(jnp.float32)
                at_out = pl.ds(pl.multiple_of(i * feat + j * tile, tile), tile)
                result[:, at_out] = (top / (scaling + damping)).astype(result.dtype)

            store(i).start()

        blocks_within(low, high, block)

    own_out = pltpu.make_async_copy(og, held.at[OUT, m], load_sem.at[n_mp])
    own_in = pltpu.make_async_copy(act, held.at[IN, m], load_sem.at[n_mp + 1])
    own_grad = pltpu.make_async_copy(
        grad.at[pl.ds(pl.multiple_of(d * rows, rows), rows), :], grads.at[d], load_sem.at[n_mp + 2]
    )
    own_out.start()
    own_in.start()
    own_grad.start()
    for one in load_basis(basis_out):
        one.start()

    barrier = pltpu.get_barrier_semaphore()
    peers = [{"mp": x_peer}] + [{"dp": other} for other in others]
    for peer in peers:
        pl.semaphore_signal(barrier, inc=1, device_id=peer, device_id_type=MESH)
    for way, target in ((UP, m + 2), (DOWN, m - 2)):
        @pl.when(can_pass(way))
        def _():
            pl.semaphore_signal(barrier, inc=1, device_id={"mp": target}, device_id_type=MESH)

    inner = (z > 0).astype(jnp.int32) + (z < n_z - 1).astype(jnp.int32)
    pl.semaphore_wait(barrier, len(peers) + inner)

    def grad_copy(k, other):
        return pltpu.make_async_remote_copy(
            src_ref=grad.at[pl.ds(pl.multiple_of(other * rows, rows), rows), :], dst_ref=grads.at[d],
            send_sem=gsend.at[k], recv_sem=grecv.at[k],
            device_id={"dp": other}, device_id_type=MESH,
        )

    def in_copy(k, other):
        return pltpu.make_async_remote_copy(
            src_ref=sq_in_send.at[other], dst_ref=sq_in.at[d],
            send_sem=isend.at[k], recv_sem=irecv.at[k],
            device_id={"dp": other}, device_id_type=MESH,
        )

    own_out.wait()
    first_z(OUT)
    send_x(OUT, 0)
    for k, other in enumerate(others):
        start(True, lambda k=k, other=other: grad_copy(k, other))
    own_in.wait()
    along_z(OUT, 1)
    send_x(OUT, 1)
    from_x(OUT, 0)
    acc[...] = jnp.zeros_like(acc)
    for one in load_basis(basis_out):
        one.wait()
    pairs(OUT, 1)
    for step in range(2, n_z):
        along_z(OUT, step)
        send_x(OUT, step)
        pairs(OUT, step)
    first_z(IN)
    from_x(OUT, 1)
    multiply(OUT, 0, 1)
    from_x(OUT, 2)
    multiply(OUT, 2, 2)
    for step in range(3, n_z):
        from_x(OUT, step)
    send_x(IN, 0)
    multiply(OUT, 3, n_z)
    squares[d, m] = (acc[...] * acc[...]).astype(jnp.bfloat16)

    first_z(SQ)
    send_x(SQ, 0)
    for h in (0, 1):
        spread(0, UP, 0, h, True)
    for one in load_basis(basis_in):
        one.start()
    acc[...] = jnp.zeros_like(acc)

    along_z(SQ, 1)
    send_x(SQ, 1)
    along_z(IN, 1)
    from_x(IN, 0)
    from_x(SQ, 0)
    send_x(IN, 1)
    for step in range(2, n_z):
        along_z(SQ, step)
        along_z(IN, step)
        send_x(IN, step)
        pairs(IN, step - 1)
        pairs(SQ, step - 1)
        if step == 2:
            from_x(SQ, 1)
            from_y(0)
    for step in range(2, n_z):
        send_x(SQ, step)
        if step == 2:
            for h in (0, 1):
                start(True, lambda h=h: d_copy(h))
    pairs(IN, n_z - 1)
    pairs(SQ, n_z - 1)
    for one in load_basis(basis_in):
        one.wait()
    from_x(IN, 1)
    multiply(IN, 0, 1)
    for step in range(2, n_z):
        from_x(IN, step)
    multiply(IN, 2, n_z)
    for k in range(n_dp):
        piece = acc[:, k * rows:(k + 1) * rows]
        sq_in_send[k] = (piece * piece).T.astype(jnp.bfloat16)
    for k, other in enumerate(others):
        start(True, lambda k=k, other=other: in_copy(k, other))
    sq_in[d] = sq_in_send[d]
    from_x(SQ, 2)
    from_y(1)
    for h in (0, 1):
        arrived(True, lambda: d_copy(h, 1))
        start(True, lambda h=h: c_copy(0, UP, 1, h, 1, y_peer))
    for step in range(3, n_z):
        from_x(SQ, step)

    own_grad.wait()
    for k in range(n_dp - 1):
        back = (d + n_dp - k - 1) % n_dp
        remote(grads.at[back], gsend.at[k], grecv.at[k], {"dp": others[k]}).wait_recv()
        remote(sq_in.at[back], isend.at[k], irecv.at[k], {"dp": others[k]}).wait_recv()
    from_core(0)
    from_core(1)
    finish(0, 1)
    for step in range(2, n_z):
        from_y(step)
        from_core(step)
        finish(step, step)

    for i in range(n_mp):
        store(i).wait()
    for wanted, copy in started:
        do(wanted, lambda: copy().wait_send())


def per_device(activations, out_grads, basis_in, basis_out, grad_eigen):
    tok, feat = activations.shape
    n_dp, n_mp = lax.axis_size("dp"), lax.axis_size("mp")
    depth, cols = basis_in.shape
    height, width = grad_eigen.shape
    rows = height // n_dp
    n_z = n_mp // 2
    dma = pltpu.SemaphoreType.DMA
    spec = pl.BlockSpec(memory_space=pl.ANY)
    return pl.pallas_call(
        kernel,
        out_shape=jax.ShapeDtypeStruct((rows, depth), jnp.bfloat16),
        in_specs=[spec] * 5,
        out_specs=spec,
        scratch_shapes=[
            pltpu.VMEM((2, n_mp, tok, feat), jnp.bfloat16),
            pltpu.VMEM((n_dp, n_mp, tok, cols), jnp.bfloat16),
            pltpu.VMEM((n_dp, rows, tok), jnp.bfloat16),
            pltpu.VMEM((n_dp, rows, tok), jnp.bfloat16),
            pltpu.VMEM((n_dp, rows, width), jnp.bfloat16),
            pltpu.VMEM((n_mp, feat, cols), jnp.bfloat16),
            pltpu.VMEM((tok, cols), jnp.float32),
            pltpu.VMEM((rows, depth), jnp.bfloat16),
            dma((n_mp + 3,)), dma((n_mp,)),
            dma((3, n_z - 1, 2, 2, 2)), dma((3, n_z - 1, 2, 2, 2)),
            dma((3, n_z, 2, 2)), dma((3, n_z, 2, 2)),
            dma((2,)), dma((2,)),
            dma((n_z, 2, 2, 2)), dma((n_z, 2, 2, 2)),
            dma((2, n_z, 2, 2, 2)), dma((2, n_z, 2, 2, 2)),
            dma((n_dp,)), dma((n_dp,)),
            dma((n_dp,)), dma((n_dp,)),
        ],
        compiler_params=pltpu.CompilerParams(
            collective_id=0, has_side_effects=True, vmem_limit_bytes=60 * 1024 * 1024
        ),
        cost_estimate=pl.CostEstimate(
            flops=4 * tok * depth * cols + 2 * rows * tok * n_dp * depth,
            bytes_accessed=4 * depth * cols + 4 * height * width,
            transcendentals=0,
        ),
    )(activations, out_grads, basis_in, basis_out, grad_eigen)


def solution(mesh):
    placed = (P("dp", "mp"), P("dp", "mp"), P(None, "mp"), P(None, "mp"), P("mp", "dp"))
    routed = (mesh.shape["dp"], mesh.shape["mp"]) == (4, 8)
    return jax.shard_map(
        per_device if routed else general,
        mesh=mesh, in_specs=placed, out_specs=P(("mp", "dp"), None), check_vma=False,
    )
```

```python
import jax
import jax.numpy as jnp
from jax import lax
from jax.experimental import pallas as pl
from jax.experimental.pallas import tpu as pltpu
from jax.sharding import PartitionSpec as P

damping = 0.1
MESH = pl.DeviceIdType.MESH
OUT, IN, SQ = 0, 1, 2
UP, DOWN = 0, 1


def projector(basis, piece):
    return jnp.dot(piece, basis, preferred_element_type=jnp.float32)


def general(activations, out_grads, basis_in, basis_out, grad_eigen):
    tok_rows = activations.shape[0]
    groups = lax.axis_size("dp")
    proj_in = projector(basis_in, lax.all_gather(activations, "mp", axis=1, tiled=True))
    proj_out = projector(basis_out, lax.all_gather(out_grads, "mp", axis=1, tiled=True))
    squares_in = (proj_in * proj_in).astype(jnp.bfloat16)
    squares_out = (proj_out * proj_out).astype(jnp.bfloat16)
    partial_sums = lax.dot_general(
        squares_in,
        lax.all_gather(squares_out, "mp", axis=1, tiled=True),
        (((0,), (0,)), ((), ())),
        preferred_element_type=jnp.float32,
    )
    summed = lax.psum_scatter(
        partial_sums.astype(jnp.bfloat16), "dp", scatter_dimension=1, tiled=True
    ).astype(jnp.float32)
    scaling = summed / (tok_rows * groups)
    block_result = (grad_eigen.astype(jnp.float32) / (scaling + damping)).astype(jnp.bfloat16)
    return lax.all_to_all(block_result, "dp", split_axis=0, concat_axis=1, tiled=True)


def kernel(
    act, og, basis_in, basis_out, grad, out,
    held, squares, sq_in, sq_in_send, sq_all, grads, basis, acc, result,
    load_sem, store_sem, zsend, zrecv, xsend, xrecv, dsend, drecv, ysend, yrecv, csend, crecv,
    gsend, grecv, isend, irecv,
):
    tok, feat = act.shape
    n_mp, n_dp = held.shape[1], sq_in.shape[0]
    n_z = n_mp // 2
    rows = out.shape[0]
    width = grad.shape[1]
    half = tok // 2
    d, m = lax.axis_index("dp"), lax.axis_index("mp")
    y, c = d // 2, d % 2
    z, x = m // 2, m % 2
    y_peer, c_peer, x_peer = (1 - y) * 2 + c, y * 2 + 1 - c, z * 2 + 1 - x
    diagonal = (1 - y) * 2 + 1 - c
    others = [(d + i) % n_dp for i in range(1, n_dp)]
    started = []

    def do(wanted, action):
        if wanted is True:
            action()
        else:
            pl.when(wanted)(action)

    def start(wanted, copy):
        started.append((wanted, copy))
        do(wanted, lambda: copy().start())

    def arrived(wanted, copy):
        do(wanted, lambda: copy().wait_recv())

    def both(one, other):
        if one is True:
            return other
        return one if other is True else one & other

    def slot_of(step, way, other_x):
        at = z - step if way == UP else z + step
        return at * 2 + ((1 - x) if other_x else x)

    def there(step, way):
        if step == 0:
            return True
        return z >= step if way == UP else z + step < n_z

    def ways(step):
        return (UP,) if step == 0 else (UP, DOWN)

    def can_pass(way):
        return z < n_z - 1 if way == UP else z > 0

    def paired(step, way, h):
        if h == 0 or step == 0:
            return False
        return z == step if way == UP else z + step == n_z - 1

    def alone(step, way, h):
        if h == 0 or step == 0:
            return there(step, way)
        return z > step if way == UP else z + step < n_z - 1

    def part(a, step, way, other_x, h, owner=None):
        slot = slot_of(step, way, other_x)
        if a == SQ:
            lines = (d if owner is None else owner) * tok + h * half
            return squares.at[slot, pl.ds(pl.multiple_of(lines, half), half)]
        return held.at[a, slot, pl.ds(h * half, half)]

    def remote(ref, send, recv, target):
        return pltpu.make_async_remote_copy(
            src_ref=ref, dst_ref=ref, send_sem=send, recv_sem=recv,
            device_id=target, device_id_type=MESH,
        )

    def z_copy(a, step, way, other_x, h):
        at = (a, step, way, other_x, h)
        target = m + 2 if way == UP else m - 2
        return remote(part(*at), zsend.at[at], zrecv.at[at], {"mp": target})

    def x_copy(a, step, way, h, other_x=0):
        at = (a, step, way, h)
        return remote(part(a, step, way, other_x, h), xsend.at[at], xrecv.at[at], {"mp": x_peer})

    def d_copy(h, other_x=0):
        return remote(part(SQ, 0, UP, other_x, h, y_peer), dsend.at[h], drecv.at[h], {"mp": x_peer})

    def y_copy(step, way, other_x, h, owner):
        at = (step, way, other_x, h)
        return remote(part(SQ, *at, owner), ysend.at[at], yrecv.at[at], {"dp": y_peer})

    def c_copy(step, way, other_x, h, far, owner):
        at = (step, way, other_x, h)
        return remote(part(SQ, *at, owner), csend.at[(far,) + at], crecv.at[(far,) + at], {"dp": c_peer})

    def send_z(a, step, way, other_x, h, wanted):
        if step < n_z - 1:
            start(both(wanted, can_pass(way)), lambda: z_copy(a, step, way, other_x, h))

    def send_x(a, step):
        for h in (0, 1):
            for way in ways(step):
                start(alone(step, way, h), lambda way=way, h=h: x_copy(a, step, way, h))

    def spread(step, way, other_x, h, wanted):
        if step > 0 or not other_x:
            start(wanted, lambda: y_copy(step, way, other_x, h, d))
        start(wanted, lambda: c_copy(step, way, other_x, h, 0, d))

    def first_z(a):
        for h in (0, 1):
            for way in (UP, DOWN):
                send_z(a, 0, way, 0, h, True)

    def along_z(a, step):
        for h in (0, 1):
            for way in (UP, DOWN):
                wanted = there(step, way)
                arrived(wanted, lambda: z_copy_in(a, step, way, 0, h))
                send_z(a, step, way, 0, h, wanted)
                if a == SQ:
                    spread(step, way, 0, h, wanted)

    def z_copy_in(a, step, way, other_x, h):
        ref = part(a, step, way, other_x, h)
        at = (a, step - 1, way, other_x, h)
        return remote(ref, zsend.at[at], zrecv.at[at], {"mp": x_peer})

    def pairs(a, step):
        for way in (UP, DOWN):
            wanted = paired(step, way, 1)
            arrived(wanted, lambda: z_copy_in(a, step, way, 1, 1))
            send_z(a, step, way, 1, 1, wanted)
            if a == SQ:
                spread(step, way, 1, 1, wanted)

    def from_x(a, step):
        for h in (0, 1):
            for way in ways(step):
                wanted = alone(step, way, h)
                arrived(wanted, lambda: x_copy(a, step, way, h, 1))
                if step == 0 and h == 1:
                    send_z(a, 0, UP, 1, h, z == 0)
                    send_z(a, 0, DOWN, 1, h, z == n_z - 1)
                if a == SQ:
                    spread(step, way, 1, h, wanted)

    def from_y(step):
        for other_x in (0, 1) if step > 0 else (0,):
            for h in (0, 1):
                for way in ways(step):
                    wanted = there(step, way)
                    arrived(wanted, lambda: y_copy(step, way, other_x, h, y_peer))
                    start(wanted, lambda way=way, other_x=other_x, h=h: c_copy(step, way, other_x, h, 1, y_peer))

    def from_core(step):
        for other_x in (0, 1):
            for h in (0, 1):
                for way in ways(step):
                    wanted = there(step, way)
                    arrived(wanted, lambda: c_copy(step, way, other_x, h, 0, c_peer))
                    arrived(wanted, lambda: c_copy(step, way, other_x, h, 1, diagonal))

    def load_basis(source):
        return [
            pltpu.make_async_copy(source.at[pl.ds(i * feat, feat), :], basis.at[i], load_sem.at[i])
            for i in range(n_mp)
        ]

    tile = 256

    def blocks_within(low, high, action):
        def one(i, carry):
            away = jnp.abs(i // 2 - z)
            pl.when((away >= low) & (away <= high))(lambda: action(i))
            return carry

        lax.fori_loop(0, n_mp, one, 0)

    def multiply(a, low, high):
        def block(i):
            @pl.loop(0, acc.shape[1] // tile)
            def _(j):
                cols = pl.ds(pl.multiple_of(j * tile, tile), tile)
                acc[:, cols] += jnp.dot(held[a, i], basis[i, :, cols], preferred_element_type=jnp.float32)

        blocks_within(low, high, block)

    def store(i):
        cols = pl.ds(pl.multiple_of(i * feat, feat), feat)
        return pltpu.make_async_copy(result.at[:, cols], out.at[:, cols], store_sem.at[i])

    def finish(low, high):
        per_grad = width // feat

        def block(i):
            @pl.loop(0, feat // tile)
            def _(j):
                cols = pl.ds(pl.multiple_of(j * tile, tile), tile)
                total = jnp.dot(sq_all[...], squares[i, :, cols], preferred_element_type=jnp.float32)
                scaling = total / (tok * n_dp)
                at_grad = pl.ds(pl.multiple_of((i % per_grad) * feat + j * tile, tile), tile)
                top = grads[i // per_grad, :, at_grad].astype(jnp.float32)
                at_out = pl.ds(pl.multiple_of(i * feat + j * tile, tile), tile)
                result[:, at_out] = (top / (scaling + damping)).astype(result.dtype)

            store(i).start()

        blocks_within(low, high, block)

    own_out = pltpu.make_async_copy(og, held.at[OUT, m], load_sem.at[n_mp])
    own_in = pltpu.make_async_copy(act, held.at[IN, m], load_sem.at[n_mp + 1])
    own_grad = pltpu.make_async_copy(
        grad.at[pl.ds(pl.multiple_of(d * rows, rows), rows), :], grads.at[d], load_sem.at[n_mp + 2]
    )
    own_out.start()
    own_in.start()
    own_grad.start()
    for one in load_basis(basis_out):
        one.start()

    barrier = pltpu.get_barrier_semaphore()
    peers = [{"mp": x_peer}] + [{"dp": other} for other in others]
    for peer in peers:
        pl.semaphore_signal(barrier, inc=1, device_id=peer, device_id_type=MESH)
    for way, target in ((UP, m + 2), (DOWN, m - 2)):
        @pl.when(can_pass(way))
        def _():
            pl.semaphore_signal(barrier, inc=1, device_id={"mp": target}, device_id_type=MESH)

    inner = (z > 0).astype(jnp.int32) + (z < n_z - 1).astype(jnp.int32)
    pl.semaphore_wait(barrier, len(peers) + inner)

    def grad_copy(k, other):
        return pltpu.make_async_remote_copy(
            src_ref=grad.at[pl.ds(pl.multiple_of(other * rows, rows), rows), :], dst_ref=grads.at[d],
            send_sem=gsend.at[k], recv_sem=grecv.at[k],
            device_id={"dp": other}, device_id_type=MESH,
        )

    def in_copy(k, other):
        return pltpu.make_async_remote_copy(
            src_ref=sq_in_send.at[other], dst_ref=sq_in.at[d],
            send_sem=isend.at[k], recv_sem=irecv.at[k],
            device_id={"dp": other}, device_id_type=MESH,
        )

    own_out.wait()
    first_z(OUT)
    send_x(OUT, 0)
    for k, other in enumerate(others):
        start(True, lambda k=k, other=other: grad_copy(k, other))
    own_in.wait()
    along_z(OUT, 1)
    send_x(OUT, 1)
    from_x(OUT, 0)
    acc[...] = jnp.zeros_like(acc)
    for one in load_basis(basis_out):
        one.wait()
    pairs(OUT, 1)
    multiply(OUT, 0, 0)
    for step in range(2, n_z):
        along_z(OUT, step)
        send_x(OUT, step)
        pairs(OUT, step)
    first_z(IN)
    from_x(OUT, 1)
    multiply(OUT, 1, 1)
    from_x(OUT, 2)
    multiply(OUT, 2, 2)
    for step in range(3, n_z):
        from_x(OUT, step)
    send_x(IN, 0)
    multiply(OUT, 3, n_z)
    squares[m, pl.ds(pl.multiple_of(d * tok, tok), tok)] = (acc[...] * acc[...]).astype(jnp.bfloat16)

    first_z(SQ)
    send_x(SQ, 0)
    for h in (0, 1):
        spread(0, UP, 0, h, True)
    for one in load_basis(basis_in):
        one.start()
    acc[...] = jnp.zeros_like(acc)

    along_z(SQ, 1)
    send_x(SQ, 1)
    along_z(IN, 1)
    from_x(IN, 0)
    from_x(SQ, 0)
    send_x(IN, 1)
    for one in load_basis(basis_in):
        one.wait()
    multiply(IN, 0, 0)
    for step in range(2, n_z):
        along_z(SQ, step)
        along_z(IN, step)
        send_x(IN, step)
        pairs(IN, step - 1)
        pairs(SQ, step - 1)
        if step == 2:
            from_x(SQ, 1)
            from_y(0)
    for step in range(2, n_z):
        send_x(SQ, step)
        if step == 2:
            for h in (0, 1):
                start(True, lambda h=h: d_copy(h))
    pairs(IN, n_z - 1)
    pairs(SQ, n_z - 1)
    from_x(IN, 1)
    multiply(IN, 1, 1)
    from_x(IN, 2)
    multiply(IN, 2, 2)
    for step in range(3, n_z):
        from_x(IN, step)
    multiply(IN, 3, n_z)
    for k in range(n_dp):
        piece = acc[:, k * rows:(k + 1) * rows]
        sq_in_send[k] = (piece * piece).T.astype(jnp.bfloat16)
    for k, other in enumerate(others):
        start(True, lambda k=k, other=other: in_copy(k, other))
    sq_in[d] = sq_in_send[d]
    from_x(SQ, 2)
    from_y(1)
    for h in (0, 1):
        arrived(True, lambda: d_copy(h, 1))
        start(True, lambda h=h: c_copy(0, UP, 1, h, 1, y_peer))
    for step in range(3, n_z):
        from_x(SQ, step)

    own_grad.wait()
    for k in range(n_dp - 1):
        back = (d + n_dp - k - 1) % n_dp
        remote(grads.at[back], gsend.at[k], grecv.at[k], {"dp": others[k]}).wait_recv()
        remote(sq_in.at[back], isend.at[k], irecv.at[k], {"dp": others[k]}).wait_recv()
    for k in range(n_dp):
        sq_all[:, k * tok:(k + 1) * tok] = sq_in[k]
    for step in range(n_z):
        if step > 1:
            from_y(step)
        from_core(step)
        finish(step, step)

    for i in range(n_mp):
        store(i).wait()
    for wanted, copy in started:
        do(wanted, lambda: copy().wait_send())


def per_device(activations, out_grads, basis_in, basis_out, grad_eigen):
    tok, feat = activations.shape
    n_dp, n_mp = lax.axis_size("dp"), lax.axis_size("mp")
    depth, cols = basis_in.shape
    height, width = grad_eigen.shape
    rows = height // n_dp
    n_z = n_mp // 2
    dma = pltpu.SemaphoreType.DMA
    spec = pl.BlockSpec(memory_space=pl.ANY)
    return pl.pallas_call(
        kernel,
        out_shape=jax.ShapeDtypeStruct((rows, depth), jnp.bfloat16),
        in_specs=[spec] * 5,
        out_specs=spec,
        scratch_shapes=[
            pltpu.VMEM((2, n_mp, tok, feat), jnp.bfloat16),
            pltpu.VMEM((n_mp, n_dp * tok, cols), jnp.bfloat16),
            pltpu.VMEM((n_dp, rows, tok), jnp.bfloat16),
            pltpu.VMEM((n_dp, rows, tok), jnp.bfloat16),
            pltpu.VMEM((rows, n_dp * tok), jnp.bfloat16),
            pltpu.VMEM((n_dp, rows, width), jnp.bfloat16),
            pltpu.VMEM((n_mp, feat, cols), jnp.bfloat16),
            pltpu.VMEM((tok, cols), jnp.float32),
            pltpu.VMEM((rows, depth), jnp.bfloat16),
            dma((n_mp + 3,)), dma((n_mp,)),
            dma((3, n_z - 1, 2, 2, 2)), dma((3, n_z - 1, 2, 2, 2)),
            dma((3, n_z, 2, 2)), dma((3, n_z, 2, 2)),
            dma((2,)), dma((2,)),
            dma((n_z, 2, 2, 2)), dma((n_z, 2, 2, 2)),
            dma((2, n_z, 2, 2, 2)), dma((2, n_z, 2, 2, 2)),
            dma((n_dp,)), dma((n_dp,)),
            dma((n_dp,)), dma((n_dp,)),
        ],
        compiler_params=pltpu.CompilerParams(
            collective_id=0, has_side_effects=True, vmem_limit_bytes=60 * 1024 * 1024
        ),
        cost_estimate=pl.CostEstimate(
            flops=4 * tok * depth * cols + 2 * rows * tok * n_dp * depth,
            bytes_accessed=4 * depth * cols + 4 * height * width,
            transcendentals=0,
        ),
    )(activations, out_grads, basis_in, basis_out, grad_eigen)


def solution(mesh):
    placed = (P("dp", "mp"), P("dp", "mp"), P(None, "mp"), P(None, "mp"), P("mp", "dp"))
    routed = (mesh.shape["dp"], mesh.shape["mp"]) == (4, 8)
    return jax.shard_map(
        per_device if routed else general,
        mesh=mesh, in_specs=placed, out_specs=P(("mp", "dp"), None), check_vma=False,
    )
```

```python
import jax
import jax.numpy as jnp
from jax import lax
from jax.experimental import pallas as pl
from jax.experimental.pallas import tpu as pltpu
from jax.sharding import PartitionSpec as P

damping = 0.1
MESH = pl.DeviceIdType.MESH
OUT, IN, SQ = 0, 1, 2
UP, DOWN = 0, 1


def projector(basis, piece):
    return jnp.dot(piece, basis, preferred_element_type=jnp.float32)


def general(activations, out_grads, basis_in, basis_out, grad_eigen):
    tok_rows = activations.shape[0]
    groups = lax.axis_size("dp")
    proj_in = projector(basis_in, lax.all_gather(activations, "mp", axis=1, tiled=True))
    proj_out = projector(basis_out, lax.all_gather(out_grads, "mp", axis=1, tiled=True))
    squares_in = (proj_in * proj_in).astype(jnp.bfloat16)
    squares_out = (proj_out * proj_out).astype(jnp.bfloat16)
    partial_sums = lax.dot_general(
        squares_in,
        lax.all_gather(squares_out, "mp", axis=1, tiled=True),
        (((0,), (0,)), ((), ())),
        preferred_element_type=jnp.float32,
    )
    summed = lax.psum_scatter(
        partial_sums.astype(jnp.bfloat16), "dp", scatter_dimension=1, tiled=True
    ).astype(jnp.float32)
    scaling = summed / (tok_rows * groups)
    block_result = (grad_eigen.astype(jnp.float32) / (scaling + damping)).astype(jnp.bfloat16)
    return lax.all_to_all(block_result, "dp", split_axis=0, concat_axis=1, tiled=True)


def kernel(
    act, og, basis_in, basis_out, grad, out,
    held, squares, sq_in, sq_in_send, sq_all, grads, basis, acc, result,
    load_sem, store_sem, zsend, zrecv, xsend, xrecv, dsend, drecv, ysend, yrecv, own_send, own_recv,
    gsend, grecv, isend, irecv, rsend, rrecv,
):
    tok, feat = act.shape
    n_mp, n_dp = held.shape[1], sq_in.shape[0]
    n_z = n_mp // 2
    rows = out.shape[0]
    half = tok // 2
    d, m = lax.axis_index("dp"), lax.axis_index("mp")
    y, c = d // 2, d % 2
    z, x = m // 2, m % 2
    y_peer, c_peer, x_peer = (1 - y) * 2 + c, y * 2 + 1 - c, z * 2 + 1 - x
    others = [(d + i) % n_dp for i in range(1, n_dp)]
    started = []

    def do(wanted, action):
        if wanted is True:
            action()
        else:
            pl.when(wanted)(action)

    def start(wanted, copy):
        started.append((wanted, copy))
        do(wanted, lambda: copy().start())

    def arrived(wanted, copy):
        do(wanted, lambda: copy().wait_recv())

    def both(one, other):
        if one is True:
            return other
        return one if other is True else one & other

    def slot_of(step, way, other_x):
        at = z - step if way == UP else z + step
        return at * 2 + ((1 - x) if other_x else x)

    def mine(step):
        return (z + step) % 2 == c

    def there(a, step, way):
        if step == 0:
            return mine(0) if a == SQ else True
        near = z >= step if way == UP else z + step < n_z
        return near & mine(step) if a == SQ else near

    def ways(step):
        return (UP,) if step == 0 else (UP, DOWN)

    def can_pass(way):
        return z < n_z - 1 if way == UP else z > 0

    def paired(a, step, way):
        return there(a, step, way) & (z == step if way == UP else z + step == n_z - 1)

    def alone(a, step, way, h):
        if h == 0 or step == 0:
            return there(a, step, way)
        return there(a, step, way) & (z > step if way == UP else z + step < n_z - 1)

    def part(a, step, way, other_x, h, owner=None):
        slot = slot_of(step, way, other_x)
        if a == SQ:
            lines = ((y if owner is None else owner) * 2 + h) * tok
            return squares.at[slot, pl.ds(pl.multiple_of(lines, tok), tok)]
        return held.at[a, slot, pl.ds(h * half, half)]

    def remote(ref, send, recv, target):
        return pltpu.make_async_remote_copy(
            src_ref=ref, dst_ref=ref, send_sem=send, recv_sem=recv,
            device_id=target, device_id_type=MESH,
        )

    def z_copy(a, step, way, other_x, h):
        at = (a, step, way, other_x, h)
        target = m + 2 if way == UP else m - 2
        return remote(part(*at), zsend.at[at], zrecv.at[at], {"mp": target})

    def x_copy(a, step, way, h, other_x=0):
        at = (a, step, way, h)
        return remote(part(a, step, way, other_x, h), xsend.at[at], xrecv.at[at], {"mp": x_peer})

    def d_copy(h, other_x=0):
        return remote(part(SQ, 0, UP, other_x, h, 1 - y), dsend.at[h], drecv.at[h], {"mp": x_peer})

    def y_copy(step, way, other_x, h, owner):
        at = (step, way, other_x, h)
        return remote(part(SQ, *at, owner), ysend.at[at], yrecv.at[at], {"dp": y_peer})

    def own_copy():
        lines = pl.ds(pl.multiple_of(d * tok, tok), tok)
        return remote(squares.at[m, lines], own_send, own_recv, {"dp": c_peer})

    def own_copy_in():
        lines = pl.ds(pl.multiple_of(c_peer * tok, tok), tok)
        return remote(squares.at[m, lines], own_send, own_recv, {"dp": c_peer})

    def send_z(a, step, way, other_x, h, wanted):
        if step < n_z - 1:
            start(both(wanted, can_pass(way)), lambda: z_copy(a, step, way, other_x, h))

    def send_x(a, step):
        for h in (0, 1):
            for way in ways(step):
                start(alone(a, step, way, h), lambda way=way, h=h: x_copy(a, step, way, h))

    def spread(step, way, other_x, h, wanted):
        if step > 0 or not other_x:
            start(wanted, lambda: y_copy(step, way, other_x, h, y))

    def first_z(a):
        for h in (0, 1):
            for way in (UP, DOWN):
                send_z(a, 0, way, 0, h, True)

    def first_squares():
        start((z % 2) != c, own_copy)
        for own in (True, False):
            if not own:
                arrived(mine(0), own_copy_in)
            for h in (0, 1):
                wanted = mine(0) & (c == h if own else c != h)
                for way in (UP, DOWN):
                    send_z(SQ, 0, way, 0, h, wanted)
                spread(0, UP, 0, h, wanted)
                start(wanted, lambda h=h: x_copy(SQ, 0, UP, h))

    def along_z(a, step):
        for h in (0, 1):
            for way in (UP, DOWN):
                wanted = there(a, step, way)
                arrived(wanted, lambda: z_copy_in(a, step, way, 0, h))
                send_z(a, step, way, 0, h, wanted)
                if a == SQ:
                    spread(step, way, 0, h, wanted)

    def z_copy_in(a, step, way, other_x, h):
        ref = part(a, step, way, other_x, h)
        at = (a, step - 1, way, other_x, h)
        return remote(ref, zsend.at[at], zrecv.at[at], {"mp": x_peer})

    def pairs(a, step):
        for way in (UP, DOWN):
            wanted = paired(a, step, way)
            arrived(wanted, lambda: z_copy_in(a, step, way, 1, 1))
            send_z(a, step, way, 1, 1, wanted)
            if a == SQ:
                spread(step, way, 1, 1, wanted)

    def from_x(a, step):
        for h in (0, 1):
            for way in ways(step):
                wanted = alone(a, step, way, h)
                arrived(wanted, lambda: x_copy(a, step, way, h, 1))
                if step == 0 and h == 1:
                    send_z(a, 0, UP, 1, h, both(wanted, z == 0))
                    send_z(a, 0, DOWN, 1, h, both(wanted, z == n_z - 1))
                if a == SQ:
                    spread(step, way, 1, h, wanted)

    def from_y(step):
        for other_x in (0, 1) if step > 0 else (0,):
            for h in (0, 1):
                for way in ways(step):
                    arrived(there(SQ, step, way), lambda: y_copy(step, way, other_x, h, 1 - y))

    def load_basis(source):
        return [
            pltpu.make_async_copy(source.at[pl.ds(i * feat, feat), :], basis.at[i], load_sem.at[i])
            for i in range(n_mp)
        ]

    tile = 256

    def blocks_within(low, high, action):
        def one(i, carry):
            away = jnp.abs(i // 2 - z)
            pl.when((away >= low) & (away <= high))(lambda: action(i))
            return carry

        lax.fori_loop(0, n_mp, one, 0)

    def multiply(a, low, high):
        def block(i):
            @pl.loop(0, acc.shape[1] // tile)
            def _(j):
                cols = pl.ds(pl.multiple_of(j * tile, tile), tile)
                acc[:, cols] += jnp.dot(held[a, i], basis[i, :, cols], preferred_element_type=jnp.float32)

        blocks_within(low, high, block)

    def place(i):
        return (i // 4) * 2 + i % 2

    def columns_of(i):
        return pl.ds(pl.multiple_of(i * feat, feat), feat)

    def store(i):
        mine_rows = pl.ds(pl.multiple_of(c * rows, rows), rows)
        return pltpu.make_async_copy(result.at[place(i), mine_rows], out.at[:, columns_of(i)], store_sem.at[place(i)])

    def hand_over(i):
        their_rows = pl.ds(pl.multiple_of((1 - c) * rows, rows), rows)
        return pltpu.make_async_remote_copy(
            src_ref=result.at[place(i), their_rows], dst_ref=out.at[:, columns_of(i)],
            send_sem=rsend.at[place(i)], recv_sem=rrecv.at[place(i)],
            device_id={"dp": c_peer}, device_id_type=MESH,
        )

    def finish(low, high):
        def block(i):
            @pl.when((i // 2) % 2 == c)
            def _():
                @pl.loop(0, feat // tile)
                def _(j):
                    cols = pl.ds(pl.multiple_of(j * tile, tile), tile)
                    total = jnp.dot(sq_all[...], squares[i, :, cols], preferred_element_type=jnp.float32)
                    scaling = total / (tok * n_dp)
                    at_grad = pl.ds(pl.multiple_of((i % 2) * feat + j * tile, tile), tile)
                    top = grads[i // 4, :, at_grad].astype(jnp.float32)
                    result[place(i), :, cols] = (top / (scaling + damping)).astype(result.dtype)

                hand_over(i).start()
                store(i).start()

        blocks_within(low, high, block)

    own_out = pltpu.make_async_copy(og, held.at[OUT, m], load_sem.at[n_mp])
    own_in = pltpu.make_async_copy(act, held.at[IN, m], load_sem.at[n_mp + 1])
    own_grad = pltpu.make_async_copy(
        grad.at[pl.ds(pl.multiple_of(y * 2 * rows, 2 * rows), 2 * rows), :], grads.at[y], load_sem.at[n_mp + 2]
    )
    own_out.start()
    own_in.start()
    own_grad.start()
    for one in load_basis(basis_out):
        one.start()

    barrier = pltpu.get_barrier_semaphore()
    peers = [{"mp": x_peer}] + [{"dp": other} for other in others]
    for peer in peers:
        pl.semaphore_signal(barrier, inc=1, device_id=peer, device_id_type=MESH)
    for way, target in ((UP, m + 2), (DOWN, m - 2)):
        @pl.when(can_pass(way))
        def _():
            pl.semaphore_signal(barrier, inc=1, device_id={"mp": target}, device_id_type=MESH)

    inner = (z > 0).astype(jnp.int32) + (z < n_z - 1).astype(jnp.int32)
    pl.semaphore_wait(barrier, len(peers) + inner)

    def grad_copy():
        return pltpu.make_async_remote_copy(
            src_ref=grad.at[pl.ds(pl.multiple_of((1 - y) * 2 * rows, 2 * rows), 2 * rows), :], dst_ref=grads.at[y],
            send_sem=gsend, recv_sem=grecv,
            device_id={"dp": y_peer}, device_id_type=MESH,
        )

    def in_copy(k, other):
        return pltpu.make_async_remote_copy(
            src_ref=sq_in_send.at[other // 2], dst_ref=sq_in.at[d],
            send_sem=isend.at[k], recv_sem=irecv.at[k],
            device_id={"dp": other}, device_id_type=MESH,
        )

    own_out.wait()
    first_z(OUT)
    send_x(OUT, 0)
    start(True, grad_copy)
    own_in.wait()
    along_z(OUT, 1)
    send_x(OUT, 1)
    from_x(OUT, 0)
    acc[...] = jnp.zeros_like(acc)
    for one in load_basis(basis_out):
        one.wait()
    pairs(OUT, 1)
    multiply(OUT, 0, 0)
    for step in range(2, n_z):
        along_z(OUT, step)
        send_x(OUT, step)
        pairs(OUT, step)
    first_z(IN)
    from_x(OUT, 1)
    multiply(OUT, 1, 1)
    from_x(OUT, 2)
    multiply(OUT, 2, 2)
    for step in range(3, n_z):
        from_x(OUT, step)
    send_x(IN, 0)
    multiply(OUT, 3, n_z)
    squares[m, pl.ds(pl.multiple_of(d * tok, tok), tok)] = (acc[...] * acc[...]).astype(jnp.bfloat16)

    first_squares()
    for one in load_basis(basis_in):
        one.start()
    acc[...] = jnp.zeros_like(acc)

    along_z(SQ, 1)
    send_x(SQ, 1)
    along_z(IN, 1)
    from_x(IN, 0)
    from_x(SQ, 0)
    send_x(IN, 1)
    for one in load_basis(basis_in):
        one.wait()
    multiply(IN, 0, 0)
    for step in range(2, n_z):
        along_z(SQ, step)
        along_z(IN, step)
        send_x(IN, step)
        pairs(IN, step - 1)
        pairs(SQ, step - 1)
        if step == 2:
            from_x(SQ, 1)
            from_y(0)
    for step in range(2, n_z):
        send_x(SQ, step)
        if step == 2:
            for h in (0, 1):
                start(mine(0), lambda h=h: d_copy(h))
    pairs(IN, n_z - 1)
    pairs(SQ, n_z - 1)
    from_x(IN, 1)
    multiply(IN, 1, 1)
    from_x(IN, 2)
    multiply(IN, 2, 2)
    for step in range(3, n_z):
        from_x(IN, step)
    multiply(IN, 3, n_z)
    for k in range(2):
        piece = acc[:, k * 2 * rows:(k + 1) * 2 * rows]
        sq_in_send[k] = (piece * piece).T.astype(jnp.bfloat16)
    for k, other in enumerate(others):
        start(True, lambda k=k, other=other: in_copy(k, other))
    sq_in[d] = sq_in_send[y]
    from_x(SQ, 2)
    from_y(1)
    for h in (0, 1):
        arrived(mine(0), lambda: d_copy(h, 1))
    for step in range(3, n_z):
        from_x(SQ, step)

    own_grad.wait()
    remote(grads.at[1 - y], gsend, grecv, {"dp": y_peer}).wait_recv()
    for k in range(n_dp - 1):
        back = (d + n_dp - k - 1) % n_dp
        remote(sq_in.at[back], isend.at[k], irecv.at[k], {"dp": others[k]}).wait_recv()
    for k in range(n_dp):
        sq_all[:, k * tok:(k + 1) * tok] = sq_in[k]
    for step in range(n_z):
        if step > 1:
            from_y(step)
        finish(step, step)

    for k in range(n_mp // 2):
        i = (k // 2) * 4 + c * 2 + k % 2
        store(i).wait()
        hand_over(i).wait_send()
        hand_over((k // 2) * 4 + (1 - c) * 2 + k % 2).wait_recv()
    for wanted, copy in started:
        do(wanted, lambda: copy().wait_send())


def per_device(activations, out_grads, basis_in, basis_out, grad_eigen):
    tok, feat = activations.shape
    n_dp, n_mp = lax.axis_size("dp"), lax.axis_size("mp")
    depth, cols = basis_in.shape
    height, width = grad_eigen.shape
    rows = height // n_dp
    n_z = n_mp // 2
    dma = pltpu.SemaphoreType.DMA
    spec = pl.BlockSpec(memory_space=pl.ANY)
    return pl.pallas_call(
        kernel,
        out_shape=jax.ShapeDtypeStruct((rows, depth), jnp.bfloat16),
        in_specs=[spec] * 5,
        out_specs=spec,
        scratch_shapes=[
            pltpu.VMEM((2, n_mp, tok, feat), jnp.bfloat16),
            pltpu.VMEM((n_mp, n_dp * tok, cols), jnp.bfloat16),
            pltpu.VMEM((n_dp, 2 * rows, tok), jnp.bfloat16),
            pltpu.VMEM((2, 2 * rows, tok), jnp.bfloat16),
            pltpu.VMEM((2 * rows, n_dp * tok), jnp.bfloat16),
            pltpu.VMEM((2, 2 * rows, width), jnp.bfloat16),
            pltpu.VMEM((n_mp, feat, cols), jnp.bfloat16),
            pltpu.VMEM((tok, cols), jnp.float32),
            pltpu.VMEM((n_mp // 2, 2 * rows, feat), jnp.bfloat16),
            dma((n_mp + 3,)), dma((n_mp // 2,)),
            dma((3, n_z - 1, 2, 2, 2)), dma((3, n_z - 1, 2, 2, 2)),
            dma((3, n_z, 2, 2)), dma((3, n_z, 2, 2)),
            dma((2,)), dma((2,)),
            dma((n_z, 2, 2, 2)), dma((n_z, 2, 2, 2)),
            dma, dma,
            dma, dma,
            dma((n_dp,)), dma((n_dp,)),
            dma((n_mp // 2,)), dma((n_mp // 2,)),
        ],
        compiler_params=pltpu.CompilerParams(
            collective_id=0, has_side_effects=True, vmem_limit_bytes=60 * 1024 * 1024
        ),
        cost_estimate=pl.CostEstimate(
            flops=4 * tok * depth * cols + 2 * rows * tok * n_dp * depth,
            bytes_accessed=4 * depth * cols + 4 * height * width,
            transcendentals=0,
        ),
    )(activations, out_grads, basis_in, basis_out, grad_eigen)


def solution(mesh):
    placed = (P("dp", "mp"), P("dp", "mp"), P(None, "mp"), P(None, "mp"), P("mp", "dp"))
    routed = (mesh.shape["dp"], mesh.shape["mp"]) == (4, 8)
    return jax.shard_map(
        per_device if routed else general,
        mesh=mesh, in_specs=placed, out_specs=P(("mp", "dp"), None), check_vma=False,
    )
```

```python
import jax
import jax.numpy as jnp
from jax import lax
from jax.experimental import pallas as pl
from jax.experimental.pallas import tpu as pltpu
from jax.sharding import PartitionSpec as P

damping = 0.1
MESH = pl.DeviceIdType.MESH
OUT, IN, SQ = 0, 1, 2
UP, DOWN = 0, 1


def projector(basis, piece):
    return jnp.dot(piece, basis, preferred_element_type=jnp.float32)


def general(activations, out_grads, basis_in, basis_out, grad_eigen):
    tok_rows = activations.shape[0]
    groups = lax.axis_size("dp")
    proj_in = projector(basis_in, lax.all_gather(activations, "mp", axis=1, tiled=True))
    proj_out = projector(basis_out, lax.all_gather(out_grads, "mp", axis=1, tiled=True))
    squares_in = (proj_in * proj_in).astype(jnp.bfloat16)
    squares_out = (proj_out * proj_out).astype(jnp.bfloat16)
    partial_sums = lax.dot_general(
        squares_in,
        lax.all_gather(squares_out, "mp", axis=1, tiled=True),
        (((0,), (0,)), ((), ())),
        preferred_element_type=jnp.float32,
    )
    summed = lax.psum_scatter(
        partial_sums.astype(jnp.bfloat16), "dp", scatter_dimension=1, tiled=True
    ).astype(jnp.float32)
    scaling = summed / (tok_rows * groups)
    block_result = (grad_eigen.astype(jnp.float32) / (scaling + damping)).astype(jnp.bfloat16)
    return lax.all_to_all(block_result, "dp", split_axis=0, concat_axis=1, tiled=True)


def kernel(
    act, og, basis_in, basis_out, grad, out,
    held, squares, sq_in, sq_in_send, sq_all, grads, basis, acc, result,
    load_sem, store_sem, zsend, zrecv, xsend, xrecv, dsend, drecv, ysend, yrecv, own_send, own_recv,
    gsend, grecv, isend, irecv, rsend, rrecv,
):
    tok, feat = act.shape
    n_mp, n_dp = held.shape[1], sq_in.shape[0]
    n_z = n_mp // 2
    rows = out.shape[0]
    half = tok // 2
    d, m = lax.axis_index("dp"), lax.axis_index("mp")
    y, c = d // 2, d % 2
    z, x = m // 2, m % 2
    y_peer, c_peer, x_peer = (1 - y) * 2 + c, y * 2 + 1 - c, z * 2 + 1 - x
    others = [(d + i) % n_dp for i in range(1, n_dp)]
    started = []

    def do(wanted, action):
        if wanted is True:
            action()
        else:
            pl.when(wanted)(action)

    def start(wanted, copy):
        started.append((wanted, copy))
        do(wanted, lambda: copy().start())

    def arrived(wanted, copy):
        do(wanted, lambda: copy().wait_recv())

    def both(one, other):
        if one is True:
            return other
        return one if other is True else one & other

    def slot_of(step, way, other_x):
        at = z - step if way == UP else z + step
        return at * 2 + ((1 - x) if other_x else x)

    def mine(step):
        return (z + step) % 2 == c

    def there(a, step, way):
        if step == 0:
            return mine(0) if a == SQ else True
        near = z >= step if way == UP else z + step < n_z
        return near & mine(step) if a == SQ else near

    def ways(step):
        return (UP,) if step == 0 else (UP, DOWN)

    def can_pass(way):
        return z < n_z - 1 if way == UP else z > 0

    def paired(a, step, way):
        return there(a, step, way) & (z == step if way == UP else z + step == n_z - 1)

    def alone(a, step, way, h):
        if h == 0 or step == 0:
            return there(a, step, way)
        return there(a, step, way) & (z > step if way == UP else z + step < n_z - 1)

    def part(a, step, way, other_x, h, owner=None):
        slot = slot_of(step, way, other_x)
        if a == SQ:
            lines = ((y if owner is None else owner) * 2 + h) * tok
            return squares.at[slot, pl.ds(pl.multiple_of(lines, tok), tok)]
        return held.at[a, slot, pl.ds(h * half, half)]

    def remote(ref, send, recv, target):
        return pltpu.make_async_remote_copy(
            src_ref=ref, dst_ref=ref, send_sem=send, recv_sem=recv,
            device_id=target, device_id_type=MESH,
        )

    def z_copy(a, step, way, other_x, h):
        at = (a, step, way, other_x, h)
        target = m + 2 if way == UP else m - 2
        return remote(part(*at), zsend.at[at], zrecv.at[at], {"mp": target})

    def x_copy(a, step, way, h, other_x=0):
        at = (a, step, way, h)
        return remote(part(a, step, way, other_x, h), xsend.at[at], xrecv.at[at], {"mp": x_peer})

    def d_copy(h, other_x=0):
        return remote(part(SQ, 0, UP, other_x, h, 1 - y), dsend.at[h], drecv.at[h], {"mp": x_peer})

    def y_copy(step, way, other_x, h, owner):
        at = (step, way, other_x, h)
        return remote(part(SQ, *at, owner), ysend.at[at], yrecv.at[at], {"dp": y_peer})

    def own_copy():
        lines = pl.ds(pl.multiple_of(d * tok, tok), tok)
        return remote(squares.at[m, lines], own_send, own_recv, {"dp": c_peer})

    def own_copy_in():
        lines = pl.ds(pl.multiple_of(c_peer * tok, tok), tok)
        return remote(squares.at[m, lines], own_send, own_recv, {"dp": c_peer})

    def send_z(a, step, way, other_x, h, wanted):
        if step < n_z - 1:
            start(both(wanted, can_pass(way)), lambda: z_copy(a, step, way, other_x, h))

    def send_x(a, step):
        for h in (0, 1):
            for way in ways(step):
                start(alone(a, step, way, h), lambda way=way, h=h: x_copy(a, step, way, h))

    def spread(step, way, other_x, h, wanted):
        if step > 0 or not other_x:
            start(wanted, lambda: y_copy(step, way, other_x, h, y))

    def first_z(a):
        for h in (0, 1):
            for way in (UP, DOWN):
                send_z(a, 0, way, 0, h, True)

    def first_squares():
        start((z % 2) != c, own_copy)
        for own in (True, False):
            if not own:
                arrived(mine(0), own_copy_in)
            for h in (0, 1):
                wanted = mine(0) & (c == h if own else c != h)
                for way in (UP, DOWN):
                    send_z(SQ, 0, way, 0, h, wanted)
                spread(0, UP, 0, h, wanted)
                start(wanted, lambda h=h: x_copy(SQ, 0, UP, h))

    def along_z(a, step):
        for h in (0, 1):
            for way in (UP, DOWN):
                wanted = there(a, step, way)
                arrived(wanted, lambda: z_copy_in(a, step, way, 0, h))
                send_z(a, step, way, 0, h, wanted)
                if a == SQ:
                    spread(step, way, 0, h, wanted)

    def z_copy_in(a, step, way, other_x, h):
        ref = part(a, step, way, other_x, h)
        at = (a, step - 1, way, other_x, h)
        return remote(ref, zsend.at[at], zrecv.at[at], {"mp": x_peer})

    def pairs(a, step):
        for way in (UP, DOWN):
            wanted = paired(a, step, way)
            arrived(wanted, lambda: z_copy_in(a, step, way, 1, 1))
            send_z(a, step, way, 1, 1, wanted)
            if a == SQ:
                spread(step, way, 1, 1, wanted)

    def from_x(a, step):
        for h in (0, 1):
            for way in ways(step):
                wanted = alone(a, step, way, h)
                arrived(wanted, lambda: x_copy(a, step, way, h, 1))
                if step == 0 and h == 1:
                    send_z(a, 0, UP, 1, h, both(wanted, z == 0))
                    send_z(a, 0, DOWN, 1, h, both(wanted, z == n_z - 1))
                if a == SQ:
                    spread(step, way, 1, h, wanted)

    def from_y(step):
        for other_x in (0, 1) if step > 0 else (0,):
            for h in (0, 1):
                for way in ways(step):
                    arrived(there(SQ, step, way), lambda: y_copy(step, way, other_x, h, 1 - y))

    def load_basis(source):
        return [
            pltpu.make_async_copy(source.at[pl.ds(i * feat, feat), :], basis.at[i], load_sem.at[i])
            for i in range(n_mp)
        ]

    tile = 256

    def blocks_within(low, high, action):
        def one(i, carry):
            away = jnp.abs(i // 2 - z)
            pl.when((away >= low) & (away <= high))(lambda: action(i))
            return carry

        lax.fori_loop(0, n_mp, one, 0)

    def multiply(a, low, high):
        def block(i):
            @pl.loop(0, acc.shape[1] // tile)
            def _(j):
                cols = pl.ds(pl.multiple_of(j * tile, tile), tile)
                acc[:, cols] += jnp.dot(held[a, i], basis[i, :, cols], preferred_element_type=jnp.float32)

        blocks_within(low, high, block)

    def place(i):
        return (i // 4) * 2 + i % 2

    def columns_of(i):
        return pl.ds(pl.multiple_of(i * feat, feat), feat)

    def store(i):
        mine_rows = pl.ds(pl.multiple_of(c * rows, rows), rows)
        return pltpu.make_async_copy(result.at[place(i), mine_rows], out.at[:, columns_of(i)], store_sem.at[place(i)])

    def hand_over(i):
        their_rows = pl.ds(pl.multiple_of((1 - c) * rows, rows), rows)
        return pltpu.make_async_remote_copy(
            src_ref=result.at[place(i), their_rows], dst_ref=out.at[:, columns_of(i)],
            send_sem=rsend.at[place(i)], recv_sem=rrecv.at[place(i)],
            device_id={"dp": c_peer}, device_id_type=MESH,
        )

    def finish(low, high):
        def block(i):
            @pl.when((i // 2) % 2 == c)
            def _():
                @pl.loop(0, feat // tile)
                def _(j):
                    cols = pl.ds(pl.multiple_of(j * tile, tile), tile)
                    total = jnp.dot(sq_all[...], squares[i, :, cols], preferred_element_type=jnp.float32)
                    scaling = total / (tok * n_dp)
                    at_grad = pl.ds(pl.multiple_of((i % 2) * feat + j * tile, tile), tile)
                    top = grads[i // 4, :, at_grad].astype(jnp.float32)
                    result[place(i), :, cols] = (top / (scaling + damping)).astype(result.dtype)

                hand_over(i).start()
                store(i).start()

        blocks_within(low, high, block)

    own_out = pltpu.make_async_copy(og, held.at[OUT, m], load_sem.at[n_mp])
    own_in = pltpu.make_async_copy(act, held.at[IN, m], load_sem.at[n_mp + 1])
    own_grad = pltpu.make_async_copy(
        grad.at[pl.ds(pl.multiple_of(y * 2 * rows, 2 * rows), 2 * rows), :], grads.at[y], load_sem.at[n_mp + 2]
    )
    own_out.start()
    own_in.start()
    own_grad.start()
    for one in load_basis(basis_out):
        one.start()

    barrier = pltpu.get_barrier_semaphore()
    peers = [{"mp": x_peer}] + [{"dp": other} for other in others]
    for peer in peers:
        pl.semaphore_signal(barrier, inc=1, device_id=peer, device_id_type=MESH)
    for way, target in ((UP, m + 2), (DOWN, m - 2)):
        @pl.when(can_pass(way))
        def _():
            pl.semaphore_signal(barrier, inc=1, device_id={"mp": target}, device_id_type=MESH)

    inner = (z > 0).astype(jnp.int32) + (z < n_z - 1).astype(jnp.int32)
    pl.semaphore_wait(barrier, len(peers) + inner)

    def grad_copy():
        return pltpu.make_async_remote_copy(
            src_ref=grad.at[pl.ds(pl.multiple_of((1 - y) * 2 * rows, 2 * rows), 2 * rows), :], dst_ref=grads.at[y],
            send_sem=gsend, recv_sem=grecv,
            device_id={"dp": y_peer}, device_id_type=MESH,
        )

    def in_copy(k):
        src = (sq_in_send.at[1 - y], sq_in_send.at[y], sq_in.at[y_peer])[k]
        dst = (sq_in.at[d], sq_in.at[d], sq_in.at[y_peer])[k]
        return pltpu.make_async_remote_copy(
            src_ref=src, dst_ref=dst, send_sem=isend.at[k], recv_sem=irecv.at[k],
            device_id={"dp": (y_peer, c_peer, c_peer)[k]}, device_id_type=MESH,
        )

    def in_copy_in(k):
        owner = (y_peer, c_peer, (1 - y) * 2 + 1 - c)[k]
        return remote(sq_in.at[owner], isend.at[k], irecv.at[k], {"dp": c_peer})

    own_out.wait()
    first_z(OUT)
    send_x(OUT, 0)
    start(True, grad_copy)
    own_in.wait()
    along_z(OUT, 1)
    send_x(OUT, 1)
    from_x(OUT, 0)
    acc[...] = jnp.zeros_like(acc)
    for one in load_basis(basis_out):
        one.wait()
    pairs(OUT, 1)
    multiply(OUT, 0, 0)
    for step in range(2, n_z):
        along_z(OUT, step)
        send_x(OUT, step)
        pairs(OUT, step)
    first_z(IN)
    from_x(OUT, 1)
    multiply(OUT, 1, 1)
    from_x(OUT, 2)
    multiply(OUT, 2, 2)
    for step in range(3, n_z):
        from_x(OUT, step)
    send_x(IN, 0)
    multiply(OUT, 3, n_z)
    squares[m, pl.ds(pl.multiple_of(d * tok, tok), tok)] = (acc[...] * acc[...]).astype(jnp.bfloat16)

    first_squares()
    for one in load_basis(basis_in):
        one.start()
    acc[...] = jnp.zeros_like(acc)

    along_z(SQ, 1)
    send_x(SQ, 1)
    along_z(IN, 1)
    from_x(IN, 0)
    from_x(SQ, 0)
    send_x(IN, 1)
    for one in load_basis(basis_in):
        one.wait()
    multiply(IN, 0, 0)
    for step in range(2, n_z):
        along_z(SQ, step)
        along_z(IN, step)
        send_x(IN, step)
        pairs(IN, step - 1)
        pairs(SQ, step - 1)
        if step == 2:
            from_x(SQ, 1)
            from_y(0)
    for step in range(2, n_z):
        send_x(SQ, step)
    for h in (0, 1):
        start(mine(0), lambda h=h: d_copy(h))
    pairs(IN, n_z - 1)
    pairs(SQ, n_z - 1)
    from_x(IN, 1)
    multiply(IN, 1, 1)
    from_x(IN, 2)
    multiply(IN, 2, 2)
    for step in range(3, n_z):
        from_x(IN, step)
    multiply(IN, 3, n_z)
    for k in range(2):
        piece = acc[:, k * 2 * rows:(k + 1) * 2 * rows]
        sq_in_send[k] = (piece * piece).T.astype(jnp.bfloat16)
    start(True, lambda: in_copy(0))
    start(True, lambda: in_copy(1))
    sq_in[d] = sq_in_send[y]
    for step in range(2, n_z):
        from_x(SQ, step)
    arrived(True, lambda: in_copy_in(0))
    start(True, lambda: in_copy(2))

    own_grad.wait()
    remote(grads.at[1 - y], gsend, grecv, {"dp": y_peer}).wait_recv()
    arrived(True, lambda: in_copy_in(1))
    arrived(True, lambda: in_copy_in(2))
    for k in range(n_dp):
        sq_all[:, k * tok:(k + 1) * tok] = sq_in[k]
    for step in range(1, n_z):
        from_y(step)
        finish(step, step)
    for h in (0, 1):
        arrived(mine(0), lambda: d_copy(h, 1))
    finish(0, 0)

    for k in range(n_mp // 2):
        i = (k // 2) * 4 + c * 2 + k % 2
        store(i).wait()
        hand_over(i).wait_send()
        hand_over((k // 2) * 4 + (1 - c) * 2 + k % 2).wait_recv()
    for wanted, copy in started:
        do(wanted, lambda: copy().wait_send())


def per_device(activations, out_grads, basis_in, basis_out, grad_eigen):
    tok, feat = activations.shape
    n_dp, n_mp = lax.axis_size("dp"), lax.axis_size("mp")
    depth, cols = basis_in.shape
    height, width = grad_eigen.shape
    rows = height // n_dp
    n_z = n_mp // 2
    dma = pltpu.SemaphoreType.DMA
    spec = pl.BlockSpec(memory_space=pl.ANY)
    return pl.pallas_call(
        kernel,
        out_shape=jax.ShapeDtypeStruct((rows, depth), jnp.bfloat16),
        in_specs=[spec] * 5,
        out_specs=spec,
        scratch_shapes=[
            pltpu.VMEM((2, n_mp, tok, feat), jnp.bfloat16),
            pltpu.VMEM((n_mp, n_dp * tok, cols), jnp.bfloat16),
            pltpu.VMEM((n_dp, 2 * rows, tok), jnp.bfloat16),
            pltpu.VMEM((2, 2 * rows, tok), jnp.bfloat16),
            pltpu.VMEM((2 * rows, n_dp * tok), jnp.bfloat16),
            pltpu.VMEM((2, 2 * rows, width), jnp.bfloat16),
            pltpu.VMEM((n_mp, feat, cols), jnp.bfloat16),
            pltpu.VMEM((tok, cols), jnp.float32),
            pltpu.VMEM((n_mp // 2, 2 * rows, feat), jnp.bfloat16),
            dma((n_mp + 3,)), dma((n_mp // 2,)),
            dma((3, n_z - 1, 2, 2, 2)), dma((3, n_z - 1, 2, 2, 2)),
            dma((3, n_z, 2, 2)), dma((3, n_z, 2, 2)),
            dma((2,)), dma((2,)),
            dma((n_z, 2, 2, 2)), dma((n_z, 2, 2, 2)),
            dma, dma,
            dma, dma,
            dma((n_dp,)), dma((n_dp,)),
            dma((n_mp // 2,)), dma((n_mp // 2,)),
        ],
        compiler_params=pltpu.CompilerParams(
            collective_id=0, has_side_effects=True, vmem_limit_bytes=60 * 1024 * 1024
        ),
        cost_estimate=pl.CostEstimate(
            flops=4 * tok * depth * cols + 2 * rows * tok * n_dp * depth,
            bytes_accessed=4 * depth * cols + 4 * height * width,
            transcendentals=0,
        ),
    )(activations, out_grads, basis_in, basis_out, grad_eigen)


def solution(mesh):
    placed = (P("dp", "mp"), P("dp", "mp"), P(None, "mp"), P(None, "mp"), P("mp", "dp"))
    routed = (mesh.shape["dp"], mesh.shape["mp"]) == (4, 8)
    return jax.shard_map(
        per_device if routed else general,
        mesh=mesh, in_specs=placed, out_specs=P(("mp", "dp"), None), check_vma=False,
    )
```

```python
import jax
import jax.numpy as jnp
from jax import lax
from jax.experimental import pallas as pl
from jax.experimental.pallas import tpu as pltpu
from jax.sharding import PartitionSpec as P

damping = 0.1
MESH = pl.DeviceIdType.MESH
OUT, IN, SQ = 0, 1, 2
UP, DOWN = 0, 1


def projector(basis, piece):
    return jnp.dot(piece, basis, preferred_element_type=jnp.float32)


def general(activations, out_grads, basis_in, basis_out, grad_eigen):
    tok_rows = activations.shape[0]
    groups = lax.axis_size("dp")
    proj_in = projector(basis_in, lax.all_gather(activations, "mp", axis=1, tiled=True))
    proj_out = projector(basis_out, lax.all_gather(out_grads, "mp", axis=1, tiled=True))
    squares_in = (proj_in * proj_in).astype(jnp.bfloat16)
    squares_out = (proj_out * proj_out).astype(jnp.bfloat16)
    partial_sums = lax.dot_general(
        squares_in,
        lax.all_gather(squares_out, "mp", axis=1, tiled=True),
        (((0,), (0,)), ((), ())),
        preferred_element_type=jnp.float32,
    )
    summed = lax.psum_scatter(
        partial_sums.astype(jnp.bfloat16), "dp", scatter_dimension=1, tiled=True
    ).astype(jnp.float32)
    scaling = summed / (tok_rows * groups)
    block_result = (grad_eigen.astype(jnp.float32) / (scaling + damping)).astype(jnp.bfloat16)
    return lax.all_to_all(block_result, "dp", split_axis=0, concat_axis=1, tiled=True)


def kernel(
    act, og, basis_in, basis_out, grad, out,
    held, squares, sq_in, sq_in_send, sq_all, grads, basis, acc, result,
    load_sem, store_sem, zsend, zrecv, xsend, xrecv, dsend, drecv, ysend, yrecv, own_send, own_recv,
    gsend, grecv, isend, irecv, rsend, rrecv,
):
    tok, feat = act.shape
    n_mp, n_dp = held.shape[1], sq_in.shape[0]
    n_z = n_mp // 2
    rows = out.shape[0]
    half = tok // 2
    d, m = lax.axis_index("dp"), lax.axis_index("mp")
    y, c = d // 2, d % 2
    z, x = m // 2, m % 2
    y_peer, c_peer, x_peer = (1 - y) * 2 + c, y * 2 + 1 - c, z * 2 + 1 - x
    others = [(d + i) % n_dp for i in range(1, n_dp)]
    started = []

    def do(wanted, action):
        if wanted is True:
            action()
        else:
            pl.when(wanted)(action)

    def start(wanted, copy):
        started.append((wanted, copy))
        do(wanted, lambda: copy().start())

    def arrived(wanted, copy):
        do(wanted, lambda: copy().wait_recv())

    def both(one, other):
        if one is True:
            return other
        return one if other is True else one & other

    def slot_of(step, way, other_x):
        at = z - step if way == UP else z + step
        return at * 2 + ((1 - x) if other_x else x)

    def mine(step):
        return (z + step) % 2 == c

    def there(a, step, way):
        if step == 0:
            return mine(0) if a == SQ else True
        near = z >= step if way == UP else z + step < n_z
        return near & mine(step) if a == SQ else near

    def ways(step):
        return (UP,) if step == 0 else (UP, DOWN)

    def can_pass(way):
        return z < n_z - 1 if way == UP else z > 0

    def paired(a, step, way):
        return there(a, step, way) & (z == step if way == UP else z + step == n_z - 1)

    def alone(a, step, way, h):
        if h == 0 or step == 0:
            return there(a, step, way)
        return there(a, step, way) & (z > step if way == UP else z + step < n_z - 1)

    def part(a, step, way, other_x, h, owner=None):
        slot = slot_of(step, way, other_x)
        if a == SQ:
            lines = ((y if owner is None else owner) * 2 + h) * tok
            return squares.at[slot, pl.ds(pl.multiple_of(lines, tok), tok)]
        return held.at[a, slot, pl.ds(h * half, half)]

    def remote(ref, send, recv, target):
        return pltpu.make_async_remote_copy(
            src_ref=ref, dst_ref=ref, send_sem=send, recv_sem=recv,
            device_id=target, device_id_type=MESH,
        )

    def z_copy(a, step, way, other_x, h):
        at = (a, step, way, other_x, h)
        target = m + 2 if way == UP else m - 2
        return remote(part(*at), zsend.at[at], zrecv.at[at], {"mp": target})

    def x_copy(a, step, way, h, other_x=0):
        at = (a, step, way, h)
        return remote(part(a, step, way, other_x, h), xsend.at[at], xrecv.at[at], {"mp": x_peer})

    def d_copy(h, other_x=0):
        return remote(part(SQ, 0, UP, other_x, h, 1 - y), dsend.at[h], drecv.at[h], {"mp": x_peer})

    def y_copy(step, way, other_x, h, owner):
        at = (step, way, other_x, h)
        return remote(part(SQ, *at, owner), ysend.at[at], yrecv.at[at], {"dp": y_peer})

    def own_copy():
        lines = pl.ds(pl.multiple_of(d * tok, tok), tok)
        return remote(squares.at[m, lines], own_send, own_recv, {"dp": c_peer})

    def own_copy_in():
        lines = pl.ds(pl.multiple_of(c_peer * tok, tok), tok)
        return remote(squares.at[m, lines], own_send, own_recv, {"dp": c_peer})

    def send_z(a, step, way, other_x, h, wanted):
        if step < n_z - 1:
            start(both(wanted, can_pass(way)), lambda: z_copy(a, step, way, other_x, h))

    def send_x(a, step):
        for h in (0, 1):
            for way in ways(step):
                start(alone(a, step, way, h), lambda way=way, h=h: x_copy(a, step, way, h))

    def spread(step, way, other_x, h, wanted):
        if step > 0 or not other_x:
            start(wanted, lambda: y_copy(step, way, other_x, h, y))

    def first_z(a):
        for h in (0, 1):
            for way in (UP, DOWN):
                send_z(a, 0, way, 0, h, True)

    def first_squares():
        start((z % 2) != c, own_copy)
        for own in (True, False):
            if not own:
                arrived(mine(0), own_copy_in)
            for h in (0, 1):
                wanted = mine(0) & (c == h if own else c != h)
                for way in (UP, DOWN):
                    send_z(SQ, 0, way, 0, h, wanted)
                spread(0, UP, 0, h, wanted)
                start(wanted, lambda h=h: x_copy(SQ, 0, UP, h))

    def along_z(a, step):
        for h in (0, 1):
            for way in (UP, DOWN):
                wanted = there(a, step, way)
                arrived(wanted, lambda: z_copy_in(a, step, way, 0, h))
                send_z(a, step, way, 0, h, wanted)
                if a == SQ:
                    spread(step, way, 0, h, wanted)

    def z_copy_in(a, step, way, other_x, h):
        ref = part(a, step, way, other_x, h)
        at = (a, step - 1, way, other_x, h)
        return remote(ref, zsend.at[at], zrecv.at[at], {"mp": x_peer})

    def pairs(a, step):
        for way in (UP, DOWN):
            wanted = paired(a, step, way)
            arrived(wanted, lambda: z_copy_in(a, step, way, 1, 1))
            send_z(a, step, way, 1, 1, wanted)
            if a == SQ:
                spread(step, way, 1, 1, wanted)

    def from_x(a, step):
        for h in (0, 1):
            for way in ways(step):
                wanted = alone(a, step, way, h)
                arrived(wanted, lambda: x_copy(a, step, way, h, 1))
                if step == 0 and h == 1:
                    send_z(a, 0, UP, 1, h, both(wanted, z == 0))
                    send_z(a, 0, DOWN, 1, h, both(wanted, z == n_z - 1))
                if a == SQ:
                    spread(step, way, 1, h, wanted)

    def from_y(step):
        for other_x in (0, 1) if step > 0 else (0,):
            for h in (0, 1):
                for way in ways(step):
                    arrived(there(SQ, step, way), lambda: y_copy(step, way, other_x, h, 1 - y))

    def load_basis(source):
        return [
            pltpu.make_async_copy(source.at[pl.ds(i * feat, feat), :], basis.at[i], load_sem.at[i])
            for i in range(n_mp)
        ]

    tile = 256

    def blocks_within(low, high, action):
        def one(i, carry):
            away = jnp.abs(i // 2 - z)
            pl.when((away >= low) & (away <= high))(lambda: action(i))
            return carry

        lax.fori_loop(0, n_mp, one, 0)

    def multiply(a, low, high):
        def block(i):
            @pl.loop(0, acc.shape[1] // tile)
            def _(j):
                cols = pl.ds(pl.multiple_of(j * tile, tile), tile)
                acc[:, cols] += jnp.dot(held[a, i], basis[i, :, cols], preferred_element_type=jnp.float32)

        blocks_within(low, high, block)

    def place(i):
        return (i // 4) * 2 + i % 2

    def columns_of(i):
        return pl.ds(pl.multiple_of(i * feat, feat), feat)

    def store(i):
        mine_rows = pl.ds(pl.multiple_of(c * rows, rows), rows)
        return pltpu.make_async_copy(result.at[place(i), mine_rows], out.at[:, columns_of(i)], store_sem.at[place(i)])

    def hand_over(i):
        their_rows = pl.ds(pl.multiple_of((1 - c) * rows, rows), rows)
        return pltpu.make_async_remote_copy(
            src_ref=result.at[place(i), their_rows], dst_ref=out.at[:, columns_of(i)],
            send_sem=rsend.at[place(i)], recv_sem=rrecv.at[place(i)],
            device_id={"dp": c_peer}, device_id_type=MESH,
        )

    def finish(low, high):
        def block(i):
            @pl.when((i // 2) % 2 == c)
            def _():
                @pl.loop(0, feat // tile)
                def _(j):
                    cols = pl.ds(pl.multiple_of(j * tile, tile), tile)
                    total = jnp.dot(sq_all[...], squares[i, :, cols], preferred_element_type=jnp.float32)
                    scaling = total / (tok * n_dp)
                    at_grad = pl.ds(pl.multiple_of((i % 2) * feat + j * tile, tile), tile)
                    top = grads[i // 4, :, at_grad].astype(jnp.float32)
                    result[place(i), :, cols] = (top / (scaling + damping)).astype(result.dtype)

                hand_over(i).start()
                store(i).start()

        blocks_within(low, high, block)

    own_out = pltpu.make_async_copy(og, held.at[OUT, m], load_sem.at[n_mp])
    own_in = pltpu.make_async_copy(act, held.at[IN, m], load_sem.at[n_mp + 1])
    own_grad = pltpu.make_async_copy(
        grad.at[pl.ds(pl.multiple_of(y * 2 * rows, 2 * rows), 2 * rows), :], grads.at[y], load_sem.at[n_mp + 2]
    )
    own_out.start()
    own_in.start()
    own_grad.start()
    for one in load_basis(basis_out):
        one.start()

    barrier = pltpu.get_barrier_semaphore()
    peers = [{"mp": x_peer}] + [{"dp": other} for other in others]
    for peer in peers:
        pl.semaphore_signal(barrier, inc=1, device_id=peer, device_id_type=MESH)
    for way, target in ((UP, m + 2), (DOWN, m - 2)):
        @pl.when(can_pass(way))
        def _():
            pl.semaphore_signal(barrier, inc=1, device_id={"mp": target}, device_id_type=MESH)

    inner = (z > 0).astype(jnp.int32) + (z < n_z - 1).astype(jnp.int32)
    pl.semaphore_wait(barrier, len(peers) + inner)

    def grad_copy():
        return pltpu.make_async_remote_copy(
            src_ref=grad.at[pl.ds(pl.multiple_of((1 - y) * 2 * rows, 2 * rows), 2 * rows), :], dst_ref=grads.at[y],
            send_sem=gsend, recv_sem=grecv,
            device_id={"dp": y_peer}, device_id_type=MESH,
        )

    def in_copy(k):
        src = (sq_in_send.at[1 - y], sq_in_send.at[y], sq_in.at[y_peer])[k]
        dst = (sq_in.at[d], sq_in.at[d], sq_in.at[y_peer])[k]
        return pltpu.make_async_remote_copy(
            src_ref=src, dst_ref=dst, send_sem=isend.at[k], recv_sem=irecv.at[k],
            device_id={"dp": (y_peer, c_peer, c_peer)[k]}, device_id_type=MESH,
        )

    def in_copy_in(k):
        owner = (y_peer, c_peer, (1 - y) * 2 + 1 - c)[k]
        return remote(sq_in.at[owner], isend.at[k], irecv.at[k], {"dp": c_peer})

    own_out.wait()
    first_z(OUT)
    send_x(OUT, 0)
    start(True, grad_copy)
    own_in.wait()
    along_z(OUT, 1)
    send_x(OUT, 1)
    from_x(OUT, 0)
    acc[...] = jnp.zeros_like(acc)
    for one in load_basis(basis_out):
        one.wait()
    pairs(OUT, 1)
    multiply(OUT, 0, 0)
    for step in range(2, n_z):
        along_z(OUT, step)
        send_x(OUT, step)
        pairs(OUT, step)
    first_z(IN)
    from_x(OUT, 1)
    multiply(OUT, 1, 1)
    from_x(OUT, 2)
    multiply(OUT, 2, 2)
    for step in range(3, n_z):
        from_x(OUT, step)
    send_x(IN, 0)
    multiply(OUT, 3, n_z)
    squares[m, pl.ds(pl.multiple_of(d * tok, tok), tok)] = (acc[...] * acc[...]).astype(jnp.bfloat16)

    first_squares()
    for one in load_basis(basis_in):
        one.start()
    acc[...] = jnp.zeros_like(acc)

    along_z(SQ, 1)
    send_x(SQ, 1)
    along_z(IN, 1)
    from_x(IN, 0)
    from_x(SQ, 0)
    send_x(IN, 1)
    for one in load_basis(basis_in):
        one.wait()
    multiply(IN, 0, 0)
    for step in range(2, n_z):
        along_z(SQ, step)
        send_x(SQ, step)
        along_z(IN, step)
        send_x(IN, step)
        from_x(SQ, step - 1)
        if step == 2:
            from_y(0)
            for h in (0, 1):
                start(mine(0), lambda h=h: d_copy(h))
        pairs(IN, step - 1)
        pairs(SQ, step - 1)
    pairs(IN, n_z - 1)
    pairs(SQ, n_z - 1)
    from_x(IN, 1)
    multiply(IN, 1, 1)
    from_x(IN, 2)
    multiply(IN, 2, 2)
    for step in range(3, n_z):
        from_x(IN, step)
    multiply(IN, 3, n_z)
    for k in range(2):
        piece = acc[:, k * 2 * rows:(k + 1) * 2 * rows]
        sq_in_send[k] = (piece * piece).T.astype(jnp.bfloat16)
    start(True, lambda: in_copy(0))
    start(True, lambda: in_copy(1))
    sq_in[d] = sq_in_send[y]
    from_x(SQ, n_z - 1)
    arrived(True, lambda: in_copy_in(0))
    start(True, lambda: in_copy(2))

    own_grad.wait()
    remote(grads.at[1 - y], gsend, grecv, {"dp": y_peer}).wait_recv()
    arrived(True, lambda: in_copy_in(1))
    arrived(True, lambda: in_copy_in(2))
    for k in range(n_dp):
        sq_all[:, k * tok:(k + 1) * tok] = sq_in[k]
    for step in range(1, n_z):
        from_y(step)
        finish(step, step)
    for h in (0, 1):
        arrived(mine(0), lambda: d_copy(h, 1))
    finish(0, 0)

    for k in range(n_mp // 2):
        i = (k // 2) * 4 + c * 2 + k % 2
        store(i).wait()
        hand_over(i).wait_send()
        hand_over((k // 2) * 4 + (1 - c) * 2 + k % 2).wait_recv()
    for wanted, copy in started:
        do(wanted, lambda: copy().wait_send())


def per_device(activations, out_grads, basis_in, basis_out, grad_eigen):
    tok, feat = activations.shape
    n_dp, n_mp = lax.axis_size("dp"), lax.axis_size("mp")
    depth, cols = basis_in.shape
    height, width = grad_eigen.shape
    rows = height // n_dp
    n_z = n_mp // 2
    dma = pltpu.SemaphoreType.DMA
    spec = pl.BlockSpec(memory_space=pl.ANY)
    return pl.pallas_call(
        kernel,
        out_shape=jax.ShapeDtypeStruct((rows, depth), jnp.bfloat16),
        in_specs=[spec] * 5,
        out_specs=spec,
        scratch_shapes=[
            pltpu.VMEM((2, n_mp, tok, feat), jnp.bfloat16),
            pltpu.VMEM((n_mp, n_dp * tok, cols), jnp.bfloat16),
            pltpu.VMEM((n_dp, 2 * rows, tok), jnp.bfloat16),
            pltpu.VMEM((2, 2 * rows, tok), jnp.bfloat16),
            pltpu.VMEM((2 * rows, n_dp * tok), jnp.bfloat16),
            pltpu.VMEM((2, 2 * rows, width), jnp.bfloat16),
            pltpu.VMEM((n_mp, feat, cols), jnp.bfloat16),
            pltpu.VMEM((tok, cols), jnp.float32),
            pltpu.VMEM((n_mp // 2, 2 * rows, feat), jnp.bfloat16),
            dma((n_mp + 3,)), dma((n_mp // 2,)),
            dma((3, n_z - 1, 2, 2, 2)), dma((3, n_z - 1, 2, 2, 2)),
            dma((3, n_z, 2, 2)), dma((3, n_z, 2, 2)),
            dma((2,)), dma((2,)),
            dma((n_z, 2, 2, 2)), dma((n_z, 2, 2, 2)),
            dma, dma,
            dma, dma,
            dma((n_dp,)), dma((n_dp,)),
            dma((n_mp // 2,)), dma((n_mp // 2,)),
        ],
        compiler_params=pltpu.CompilerParams(
            collective_id=0, has_side_effects=True, vmem_limit_bytes=60 * 1024 * 1024
        ),
        cost_estimate=pl.CostEstimate(
            flops=4 * tok * depth * cols + 2 * rows * tok * n_dp * depth,
            bytes_accessed=4 * depth * cols + 4 * height * width,
            transcendentals=0,
        ),
    )(activations, out_grads, basis_in, basis_out, grad_eigen)


def solution(mesh):
    placed = (P("dp", "mp"), P("dp", "mp"), P(None, "mp"), P(None, "mp"), P("mp", "dp"))
    routed = (mesh.shape["dp"], mesh.shape["mp"]) == (4, 8)
    return jax.shard_map(
        per_device if routed else general,
        mesh=mesh, in_specs=placed, out_specs=P(("mp", "dp"), None), check_vma=False,
    )
```
